256 devices in a mesh: dp: 4 (over x_lo, core), axial: 64 (over y, z, x_hi).
Axes of the slice: x: 4 (x_hi: 2, x_lo: 2; x = x_hi * 2 + x_lo), y: 4, z: 8, core: 2. Of those that a mesh axis runs over, the one named last changes fastest.
Arguments:
- homolog_matrix: bfloat16 [4, 512, 256, 256], P('dp', 'axial'), may hold values from -6 to 6
- couple_matrix: bfloat16 [4, 256, 256, 128], P('dp', 'axial'), may hold values from -8 to 8
- result_adjoint: bfloat16 [4, 512, 256, 256], P('dp', 'axial'), may hold values from -16 to 16
- joint_projection_matrix: bfloat16 [256, 1024], replicated, may hold values from -0.375 to 0.375
- sigmoid_shift_vector: float32 [256], replicated, may hold values from -4 to 4
- final_projection_matrix: bfloat16 [256, 256], replicated, may hold values from -0.375 to 0.375
- homolog_standardize_multiplier: float32 [256], replicated, may hold values from 0.25 to 1.75
- homolog_standardize_shift: float32 [256], replicated, may hold values from -3 to 3
- couple_standardize_multiplier: float32 [128], replicated, may hold values from 0.25 to 1.75
- couple_headshift_matrix: bfloat16 [128, 8], replicated, may hold values from -4 to 4
Outputs:
- homolog_matrix_derivative: bfloat16 [4, 512, 256, 256], P('dp', 'axial')
- couple_matrix_derivative: bfloat16 [4, 256, 256, 128], P('dp', 'axial')
- d_w_qkvg: float32 [256, 1024], replicated
- d_g_bias: float32 [256], replicated
- d_w_out: float32 [256, 256], replicated
- d_msa_gain: float32 [256], replicated
- d_msa_beta: float32 [256], replicated
- d_pair_gain: float32 [128], replicated
- d_w_bias: float32 [128, 8], replicated
The draws below stay inside these ranges and needn't reach their ends.
All inputs are finite; a program needn't handle non-finite values.
Results may differ from the reference program's by a relative error of at most 0.017.
The reference program's roundings to bfloat16 on the way count: a program that leaves them out, or rounds other values in their place, can miss the bound.
Values may be sent and summed in bfloat16 or wider, within the bound.
No kernel may reach another device: no remote copies, remote signals or barrier semaphores. Data moves between devices by JAX's collectives and lax.ppermute only.
A program may use at most 64 MiB of HBM per device.

```python
import jax
import jax.numpy as jnp
from jax import lax

FEATURE_DEPTH = 256
ATTENDER_NUMBER = 8
HEAD_DIMENSION = 32
CZ = 128
CHAIN_LENGTH = 256
WINDOW_TALLY = 4
HOMOLOG_NUMBER = 512


def draw_couple_headshift_matrix(key, part):
    key = jax.random.fold_in(key, 7)
    return jnp.clip(0.1 * jax.random.normal(key, (CZ, ATTENDER_NUMBER), jnp.float32), -0.6, 0.6).astype(jnp.bfloat16)


def draw_couple_matrix(key, part):
    key = jax.random.fold_in(key, 3)
    noise = jnp.clip(jax.random.normal(key, (WINDOW_TALLY, CHAIN_LENGTH, CHAIN_LENGTH, CZ), jnp.float32), -6.0, 6.0)
    return noise.astype(jnp.bfloat16)


def strengthened(result, own_key, source, target, parts, factor):
    owner, partner = [(jnp.arange(result.shape[axis_at]) // (result.shape[axis_at] // parts)).reshape([-1 if axis == axis_at else 1 for axis in range(result.ndim)]) for axis_at in (source, target)]
    chosen = jax.random.permutation(own_key, parts)[partner]
    strong = (owner == chosen) | (owner == (partner + parts // 2) % parts)
    return jnp.where(strong, factor * result, result)


def level_of(rng, shape, split, least, high):
    factor_of = 1.0
    for dim, shards_of in split:
        draws = jax.random.uniform(jax.random.fold_in(jax.random.fold_in(rng, 6), dim), (shards_of,), jnp.float32, least / len(split), high / len(split))
        factor_of = factor_of * jnp.repeat(jnp.exp(draws), shape[dim] // shards_of).reshape((-1,) + (1,) * (len(shape) - 1 - dim))
    return factor_of


def normal_values(own_key, extent, width, bound, split=(), kind=jnp.bfloat16):
    result = width * jax.random.normal(own_key, extent, jnp.float32)
    if split:
        result = result * level_of(own_key, extent, split, -0.22, 0.18)
    return jnp.clip(result, -bound, bound).astype(kind)


def gaussian_with(rng, dims, spread, bound, cuts, heavy, kind=jnp.bfloat16):
    result = spread * jax.random.normal(rng, dims, jnp.float32)
    if cuts:
        result = result * level_of(rng, dims, cuts, -0.22, 0.18)
    return jnp.clip(strengthened(result, jax.random.fold_in(rng, 3), *heavy), -bound, bound).astype(kind)


def setup_inputs(seed: int = 0) -> dict:
    key_of = jax.random.split(jax.random.key(seed), 11)
    return {
        "homolog_matrix": normal_values(key_of[0], (WINDOW_TALLY, HOMOLOG_NUMBER, CHAIN_LENGTH, FEATURE_DEPTH), 1.0, 6.0, ((0, 4), (1, 64))),
        "couple_matrix": draw_couple_matrix(jax.random.fold_in(key_of[10], 71), 0),
        "result_adjoint": gaussian_with(key_of[2], (WINDOW_TALLY, HOMOLOG_NUMBER, CHAIN_LENGTH, FEATURE_DEPTH), 1.0, 16.0, ((0, 4), (1, 64)), (1, 2, 64, 4.0)),
        "joint_projection_matrix": normal_values(key_of[3], (FEATURE_DEPTH, 4 * ATTENDER_NUMBER * HEAD_DIMENSION), FEATURE_DEPTH ** -0.5, 0.375),
        "sigmoid_shift_vector": normal_values(key_of[4], (ATTENDER_NUMBER * HEAD_DIMENSION,), 1.0, 4.0, (), jnp.float32),
        "final_projection_matrix": normal_values(key_of[5], (ATTENDER_NUMBER * HEAD_DIMENSION, FEATURE_DEPTH), (ATTENDER_NUMBER * HEAD_DIMENSION) ** -0.5, 0.375),
        "homolog_standardize_multiplier": jnp.clip(1.0 + 0.15 * jax.random.normal(key_of[6], (FEATURE_DEPTH,), jnp.float32), 0.25, 1.75),
        "homolog_standardize_shift": normal_values(key_of[7], (FEATURE_DEPTH,), 0.5, 3.0, (), jnp.float32),
        "couple_standardize_multiplier": jnp.clip(1.0 + 0.15 * jax.random.normal(key_of[8], (CZ,), jnp.float32), 0.25, 1.75),
        "couple_headshift_matrix": draw_couple_headshift_matrix(jax.random.fold_in(key_of[10], 71), 0),
    }


eps_norm = 1e-05

def apply_layer_norm(values):
    average = lax.optimization_barrier(jnp.mean(values, axis=-1, keepdims=True))
    centered = values - average
    inverse_deviation = lax.rsqrt(lax.optimization_barrier(jnp.mean(centered * centered, axis=-1, keepdims=True)) + eps_norm)
    return (centered * inverse_deviation, inverse_deviation)

def layer_norm_reverse(grad_unit, normalized_rows, inverse_deviation):
    grad_mean = lax.optimization_barrier(jnp.mean(grad_unit, axis=-1, keepdims=True))
    cross_mean = lax.optimization_barrier(jnp.mean(grad_unit * normalized_rows, axis=-1, keepdims=True))
    return inverse_deviation * (grad_unit - grad_mean - normalized_rows * cross_mean)

def pair_normed(pair_rows, couple_standardize_multiplier):
    normalized_rows, inverse_deviation = apply_layer_norm(pair_rows.astype(jnp.float32))
    normalized_input = (normalized_rows * couple_standardize_multiplier).astype(jnp.bfloat16)
    return (normalized_input, normalized_rows, inverse_deviation)

def pair_project(normalized_input, couple_headshift_matrix):
    return jnp.einsum('ijc,ch->hij', normalized_input.astype(jnp.float32), couple_headshift_matrix.astype(jnp.float32))

def pair_backward(bias_gradient, normalized_input, normalized_rows, inverse_deviation, couple_standardize_multiplier, couple_headshift_matrix):
    d_pnormed = jnp.einsum('hij,ch->ijc', bias_gradient, couple_headshift_matrix.astype(jnp.float32))
    d_wbias = jnp.einsum('ijc,hij->ch', normalized_input.astype(jnp.float32), bias_gradient)
    d_pgain = lax.optimization_barrier(jnp.sum(normalized_rows * d_pnormed, axis=(0, 1)))
    couple_matrix_derivative = layer_norm_reverse(d_pnormed * couple_standardize_multiplier, normalized_rows, inverse_deviation).astype(jnp.bfloat16)
    return (couple_matrix_derivative, d_wbias, d_pgain)

def per_row_gradients(alignment_row, row_output_gradient, complete_bias, homolog_standardize_multiplier, homolog_standardize_shift, joint_projection_matrix, sigmoid_shift_vector, final_projection_matrix):
    residue_total = alignment_row.shape[0]
    head_width = final_projection_matrix.shape[0]
    num_heads = complete_bias.shape[0]
    head_size = head_width // num_heads
    factor = head_size ** (-0.5)
    single_precision = jnp.float32
    normalized_rows, inverse_deviation = apply_layer_norm(alignment_row.astype(single_precision))
    normalized_input = (normalized_rows * homolog_standardize_multiplier + homolog_standardize_shift).astype(jnp.bfloat16)
    projected = jnp.dot(normalized_input, joint_projection_matrix, preferred_element_type=single_precision)
    queries = (projected[:, :head_width] * factor).astype(jnp.bfloat16).reshape(residue_total, num_heads, head_size)
    key_rows = projected[:, head_width:2 * head_width].astype(jnp.bfloat16).reshape(residue_total, num_heads, head_size)
    value_rows = projected[:, 2 * head_width:3 * head_width].astype(jnp.bfloat16).reshape(residue_total, num_heads, head_size)
    gating = jax.nn.sigmoid(projected[:, 3 * head_width:] + sigmoid_shift_vector)
    logits = jnp.einsum('ihd,jhd->hij', queries.astype(single_precision), key_rows.astype(single_precision)) + complete_bias
    attn = jax.nn.softmax(logits, axis=-1)
    attn_low = attn.astype(jnp.bfloat16)
    attended = jnp.einsum('hij,jhd->ihd', attn_low.astype(single_precision), value_rows.astype(single_precision)).reshape(residue_total, head_width)
    gated = (gating * attended).astype(jnp.bfloat16)
    d_gated = jnp.dot(row_output_gradient, final_projection_matrix.T, preferred_element_type=single_precision)
    d_wout = jnp.dot(gated.T, row_output_gradient, preferred_element_type=single_precision)
    d_attended = (d_gated * gating).astype(jnp.bfloat16).reshape(residue_total, num_heads, head_size)
    d_graw = d_gated * attended * gating * (1.0 - gating)
    d_attn = jnp.einsum('ihd,jhd->hij', d_attended.astype(single_precision), value_rows.astype(single_precision))
    d_values = jnp.einsum('hij,ihd->jhd', attn_low.astype(single_precision), d_attended.astype(single_precision))
    logit_gradient = attn * (d_attn - lax.optimization_barrier(jnp.sum(attn * d_attn, axis=-1, keepdims=True)))
    d_low = logit_gradient.astype(jnp.bfloat16)
    d_queries = jnp.einsum('hij,jhd->ihd', d_low.astype(single_precision), key_rows.astype(single_precision)) * factor
    d_keys = jnp.einsum('hij,ihd->jhd', d_low.astype(single_precision), queries.astype(single_precision))
    d_projected = jnp.concatenate([d_queries.reshape(residue_total, head_width), d_keys.reshape(residue_total, head_width), d_values.reshape(residue_total, head_width), d_graw], axis=1).astype(jnp.bfloat16)
    d_wqkvg = jnp.dot(normalized_input.T, d_projected, preferred_element_type=single_precision)
    normalized_gradient = jnp.dot(d_projected, joint_projection_matrix.T, preferred_element_type=single_precision)
    alignment_row_gradient = layer_norm_reverse(normalized_gradient * homolog_standardize_multiplier, normalized_rows, inverse_deviation).astype(jnp.bfloat16)
    gradient_tree = (d_wqkvg, lax.optimization_barrier(jnp.sum(d_graw, axis=0)), d_wout, lax.optimization_barrier(jnp.sum(normalized_rows * normalized_gradient, axis=0)), lax.optimization_barrier(jnp.sum(normalized_gradient, axis=0)))
    return (alignment_row_gradient, logit_gradient, gradient_tree)

def alignment_empty(joint_projection_matrix, sigmoid_shift_vector, final_projection_matrix, homolog_standardize_multiplier):
    single_precision = jnp.float32
    return (jnp.zeros(joint_projection_matrix.shape, single_precision), jnp.zeros(sigmoid_shift_vector.shape, single_precision), jnp.zeros(final_projection_matrix.shape, single_precision), jnp.zeros(homolog_standardize_multiplier.shape, single_precision), jnp.zeros(homolog_standardize_multiplier.shape, single_precision))

def reference(homolog_matrix, couple_matrix, result_adjoint, joint_projection_matrix, sigmoid_shift_vector, final_projection_matrix, homolog_standardize_multiplier, homolog_standardize_shift, couple_standardize_multiplier, couple_headshift_matrix):
    single_precision = jnp.float32

    def window_step_change(ongoing_accumulator_nest, input_tree):
        alignment_crop, pairwise_crop, crop_output_gradient = input_tree
        normalized_input, normalized_rows, inverse_deviation = pair_normed(pairwise_crop, couple_standardize_multiplier)
        complete_bias = pair_project(normalized_input, couple_headshift_matrix)

        def per_row_update(running, partial_results):
            single_row_gradient, logit_gradient, gradient_tree = per_row_gradients(partial_results[0], partial_results[1], complete_bias, homolog_standardize_multiplier, homolog_standardize_shift, joint_projection_matrix, sigmoid_shift_vector, final_projection_matrix)
            return ((running[0] + logit_gradient, jax.tree.map(jnp.add, running[1], gradient_tree)), single_row_gradient)
        initial_state = (jnp.zeros(complete_bias.shape, single_precision), alignment_empty(joint_projection_matrix, sigmoid_shift_vector, final_projection_matrix, homolog_standardize_multiplier))
        (bias_gradient, gradient_tree), stacked_row_gradients = lax.scan(per_row_update, initial_state, (alignment_crop, crop_output_gradient))
        couple_matrix_derivative, d_wbias, d_pgain = pair_backward(bias_gradient, normalized_input, normalized_rows, inverse_deviation, couple_standardize_multiplier, couple_headshift_matrix)
        ongoing_accumulator_nest = jax.tree.map(jnp.add, ongoing_accumulator_nest, gradient_tree + (d_wbias, d_pgain))
        return (ongoing_accumulator_nest, (stacked_row_gradients, couple_matrix_derivative))
    starting_accumulator_nest = alignment_empty(joint_projection_matrix, sigmoid_shift_vector, final_projection_matrix, homolog_standardize_multiplier) + (jnp.zeros(couple_headshift_matrix.shape, single_precision), jnp.zeros(couple_standardize_multiplier.shape, single_precision))
    ongoing_accumulator_nest, (homolog_matrix_derivative, couple_matrix_derivative) = lax.scan(window_step_change, starting_accumulator_nest, (homolog_matrix, couple_matrix, result_adjoint))
    homolog_multiplier_term = float(homolog_matrix.shape[0] * homolog_matrix.shape[1] * homolog_matrix.shape[2]) ** (-0.5)
    pairwise_scale_factor = float(couple_matrix.shape[0] * couple_matrix.shape[1] * couple_matrix.shape[2]) ** (-0.5)
    return (homolog_matrix_derivative, couple_matrix_derivative, ongoing_accumulator_nest[0] * homolog_multiplier_term, ongoing_accumulator_nest[1] * homolog_multiplier_term, ongoing_accumulator_nest[2] * homolog_multiplier_term, ongoing_accumulator_nest[3] * homolog_multiplier_term, ongoing_accumulator_nest[4] * homolog_multiplier_term, ongoing_accumulator_nest[6] * pairwise_scale_factor, ongoing_accumulator_nest[5] * pairwise_scale_factor)
```

```python
import jax
import jax.numpy as jnp
from jax import lax
from jax.experimental import pallas as pl
from jax.experimental.pallas import tpu as pltpu
from jax.sharding import Mesh, PartitionSpec as P

EPS = 1e-05
F32 = jnp.float32
BF16 = jnp.bfloat16
AXIAL = ("y", "z", "x_hi")
ROWS = 1536
VMEM_LIMIT = 56 * 1024 * 1024

NN = (((1,), (0,)), ((), ()))
NT = (((1,), (1,)), ((), ()))


def mm(a, b, dims=NN):
    return lax.dot_general(a, b, dims, preferred_element_type=F32)


def norm_rows(x):
    average = jnp.mean(x, axis=-1, keepdims=True)
    centered = x - average
    inverse = lax.rsqrt(jnp.mean(centered * centered, axis=-1, keepdims=True) + EPS)
    return centered * inverse, inverse


def project_kernel(
    x_ref, adj_ref, w_ref, wo_ref, gain_ref, shift_ref, gbias_ref,
    qt_ref, kt_ref, vt_ref, k_ref, v_ref, gt_ref, dgt_ref, dat_ref, wt_ref,
):
    @pl.when(pl.program_id(0) == 0)
    def _():
        wt_ref[...] = w_ref[...].astype(F32).T.astype(BF16)

    unit, _ = norm_rows(x_ref[0].astype(F32))
    xn = (unit * gain_ref[...] + shift_ref[...]).astype(BF16)
    factor = 32 ** (-0.5)
    qt_ref[0] = (mm(wt_ref[0:256, :], xn, NT) * factor).astype(BF16)
    kt_ref[0] = mm(wt_ref[256:512, :], xn, NT).astype(BF16)
    vt_ref[0] = mm(wt_ref[512:768, :], xn, NT).astype(BF16)
    k_ref[0] = mm(xn, w_ref[:, 256:512]).astype(BF16)
    v_ref[0] = mm(xn, w_ref[:, 512:768]).astype(BF16)
    gate = jax.nn.sigmoid(mm(wt_ref[768:1024, :], xn, NT) + gbias_ref[...])
    dgated = mm(wo_ref[...], adj_ref[0], NT)
    gt_ref[0] = gate
    dgt_ref[0] = dgated
    dat_ref[0] = (dgated * gate).astype(BF16)


def project(x, adj, w, wo, gain, shift, gbias):
    rows = x.shape[0]
    block = pl.BlockSpec((1, 256, 256), lambda s: (s, 0, 0))
    whole = lambda a: pl.BlockSpec(a.shape, lambda s: (0,) * a.ndim)
    small = jax.ShapeDtypeStruct((rows, 256, 256), BF16)
    big = jax.ShapeDtypeStruct((rows, 256, 256), F32)
    return pl.pallas_call(
        project_kernel,
        grid=(rows,),
        in_specs=[block, block, whole(w), whole(wo), whole(gain), whole(shift), whole(gbias)],
        out_specs=[block] * 8,
        out_shape=[small] * 5 + [big, big, small],
        scratch_shapes=[pltpu.VMEM((1024, 256), BF16)],
        compiler_params=pltpu.CompilerParams(vmem_limit_bytes=VMEM_LIMIT),
        name="project",
    )(x, adj, w, wo, gain, shift, gbias)


def attend_kernel(
    heads, first, rows,
    bias_ref, qt_ref, kt_ref, vt_ref, k_ref, v_ref, gt_ref, dgt_ref, dat_ref,
    dp_ref, gated_ref, dbias_ref, gb_ref, bt_ref, acc_ref, out_ref,
):
    step = pl.program_id(0)

    @pl.when(step == 0)
    def _():
        for h in range(heads):
            for side in range(2):
                part = bias_ref[pl.ds(side * heads + h, 256, stride=2 * heads), :]
                bt_ref[h, 128 * side : 128 * side + 128, :] = part.T
        acc_ref[...] = jnp.zeros_like(acc_ref)
        gb_ref[...] = jnp.zeros_like(gb_ref)

    def own(block, at):
        parts = []
        if at:
            parts.append(jnp.zeros((32 * at, 256), BF16))
        parts.append(block)
        if at < 3:
            parts.append(jnp.zeros((32 * (3 - at), 256), BF16))
        return jnp.concatenate(parts, axis=0)

    for h in range(heads):
        head = first + h
        group, at = head // 4, head % 4
        lanes = slice(128 * group, 128 * group + 128)
        here = slice(32 * head, 32 * head + 32)
        out = slice(32 * h, 32 * h + 32)
        qt = qt_ref[0, here, :]
        kt = kt_ref[0, here, :]
        vt = vt_ref[0, here, :]
        dat = dat_ref[0, here, :]
        st = mm(k_ref[0, :, lanes], own(qt, at)) + bt_ref[h]
        e = jnp.exp(st - jnp.max(st, axis=0, keepdims=True))
        p = e * (1.0 / jnp.sum(e, axis=0, keepdims=True))
        p_low = p.astype(BF16)
        dpt = mm(v_ref[0, :, lanes], own(dat, at))
        delta = jnp.sum(p * dpt, axis=0, keepdims=True)
        ds = p * (dpt - delta)
        acc_ref[h] += ds
        ds_low = ds.astype(BF16)
        att = mm(vt, p_low)
        g = gt_ref[0, here, :]
        graw = dgt_ref[0, here, :] * att * g * (1.0 - g)
        gated_ref[0, out, :] = (g * att).astype(BF16)
        gb_ref[out, :] += graw[:, :128] + graw[:, 128:]
        dp_ref[0, 0, out, :] = (mm(kt, ds_low) * (32 ** (-0.5))).astype(BF16)
        dp_ref[0, 1, out, :] = mm(qt, ds_low, NT).astype(BF16)
        dp_ref[0, 2, out, :] = mm(dat, p_low, NT).astype(BF16)
        dp_ref[0, 3, out, :] = graw.astype(BF16)

    @pl.when(step == rows - 1)
    def _():
        for h in range(heads):
            for side in range(2):
                part = acc_ref[h, 128 * side : 128 * side + 128, :]
                out_ref[pl.ds(side * heads + h, 256, stride=2 * heads), :] = part.T
        dbias_ref[...] = out_ref[...].astype(BF16)


def attend(bias, qt, kt, vt, k, v, gt, dgt, dat, first, heads):
    rows = qt.shape[0]
    block = pl.BlockSpec((1, 256, 256), lambda s: (s, 0, 0))
    width = 32 * heads

    def kernel(*refs):
        attend_kernel(heads, first, rows, *refs)

    return pl.pallas_call(
        kernel,
        grid=(rows,),
        in_specs=[pl.BlockSpec((512 * heads, 128), lambda s: (0, 0))] + [block] * 8,
        out_specs=[
            pl.BlockSpec((1, 4, width, 256), lambda s: (s, 0, 0, 0)),
            pl.BlockSpec((1, width, 256), lambda s: (s, 0, 0)),
            pl.BlockSpec((512 * heads, 128), lambda s: (0, 0)),
            pl.BlockSpec((width, 128), lambda s: (0, 0)),
        ],
        out_shape=[
            jax.ShapeDtypeStruct((rows, 4, width, 256), BF16),
            jax.ShapeDtypeStruct((rows, width, 256), BF16),
            jax.ShapeDtypeStruct((512 * heads, 128), BF16),
            jax.ShapeDtypeStruct((width, 128), F32),
        ],
        scratch_shapes=[
            pltpu.VMEM((heads, 256, 256), F32),
            pltpu.VMEM((heads, 256, 256), F32),
            pltpu.VMEM((512 * heads, 128), F32),
        ],
        compiler_params=pltpu.CompilerParams(vmem_limit_bytes=VMEM_LIMIT),
        name="attend",
    )(bias, qt, kt, vt, k, v, gt, dgt, dat)


def finish_kernel(
    rows, x_ref, adj_ref, w_ref, gain_ref, shift_ref, gb_ref, dp_ref, gated_ref,
    dx_ref, grad_ref, acc_ref, wo_ref, mg_ref, mb_ref,
):
    step = pl.program_id(0)

    @pl.when(step == 0)
    def _():
        acc_ref[...] = jnp.zeros_like(acc_ref)
        wo_ref[...] = jnp.zeros_like(wo_ref)
        mg_ref[...] = jnp.zeros_like(mg_ref)
        mb_ref[...] = jnp.zeros_like(mb_ref)

    unit, inverse = norm_rows(x_ref[0].astype(F32))
    gain = gain_ref[...]
    xn = (unit * gain + shift_ref[...]).astype(BF16)
    dp = dp_ref[0]
    acc_ref[...] += mm(dp, xn)
    wo_ref[...] += mm(gated_ref[0], adj_ref[0])
    dn = mm(w_ref[...], dp).T
    mg_ref[...] += jnp.sum(unit * dn, axis=0, keepdims=True)
    mb_ref[...] += jnp.sum(dn, axis=0, keepdims=True)
    g = dn * gain
    mean = jnp.mean(g, axis=-1, keepdims=True)
    cross = jnp.mean(g * unit, axis=-1, keepdims=True)
    dx_ref[0] = (inverse * (g - mean - unit * cross)).astype(BF16)

    @pl.when(step == rows - 1)
    def _():
        gb = jnp.sum(gb_ref[...].T, axis=0, keepdims=True)
        vectors = jnp.concatenate([gb, mg_ref[...], mb_ref[...], jnp.zeros((5, 256), F32)], axis=0)
        for side in range(2):
            lanes = slice(128 * side, 128 * side + 128)
            grad_ref[side, 0:1024, :] = acc_ref[:, lanes]
            grad_ref[side, 1024:1280, :] = wo_ref[:, lanes]
            grad_ref[side, 1280:1288, :] = vectors[:, lanes]
            grad_ref[side, 1288:ROWS, :] = jnp.zeros((ROWS - 1288, 128), F32)


def finish(x, adj, w, gain, shift, gb, dp, gated):
    rows = x.shape[0]
    block = pl.BlockSpec((1, 256, 256), lambda s: (s, 0, 0))
    whole = lambda a: pl.BlockSpec(a.shape, lambda s: (0,) * a.ndim)

    def kernel(*refs):
        finish_kernel(rows, *refs)

    return pl.pallas_call(
        kernel,
        grid=(rows,),
        in_specs=[
            block, block, whole(w), whole(gain), whole(shift), whole(gb),
            pl.BlockSpec((1, 1024, 256), lambda s: (s, 0, 0)), block,
        ],
        out_specs=[block, pl.BlockSpec((2, ROWS, 128), lambda s: (0, 0, 0))],
        out_shape=[
            jax.ShapeDtypeStruct((rows, 256, 256), BF16),
            jax.ShapeDtypeStruct((2, ROWS, 128), F32),
        ],
        scratch_shapes=[
            pltpu.VMEM((1024, 256), F32),
            pltpu.VMEM((256, 256), F32),
            pltpu.VMEM((1, 256), F32),
            pltpu.VMEM((1, 256), F32),
        ],
        compiler_params=pltpu.CompilerParams(vmem_limit_bytes=VMEM_LIMIT),
        name="finish",
    )(x, adj, w, gain, shift, gb, dp, gated)


def local(x, pair, adj, w, gbias, wo, gain, shift, pair_gain, pair_w):
    x, adj, pair = x[0], adj[0], pair[0]
    unit, inverse = norm_rows(pair.astype(F32))
    pn = (unit * pair_gain).astype(BF16)
    own = jnp.einsum("ijc,ch->ihj", pn, pair_w, preferred_element_type=F32)
    own = own.reshape(4, 8, 2, 128).transpose(0, 2, 1, 3).reshape(64, 128)
    bias = own
    for axis in ("x_hi", "z", "y"):
        bias = lax.all_gather(bias, axis, tiled=True)

    gain2, shift2 = gain.reshape(1, 256), shift.reshape(1, 256)
    qt, kt, vt, k, v, gt, dgt, dat = project(x, adj, w, wo, gain2, shift2, gbias.reshape(256, 1))
    dp, gated, dbias, gb = attend(bias, qt, kt, vt, k, v, gt, dgt, dat, 0, 8)
    dx, grad = finish(x, adj, w, gain2, shift2, gb, dp.reshape(8, 1024, 256), gated)

    blocks = lax.all_to_all(dbias, AXIAL, 0, 0, tiled=True)
    d_local = jnp.sum(blocks.reshape(64, 64, 128).astype(F32), axis=0)
    d_local = d_local.reshape(4, 2, 8, 128).transpose(0, 2, 1, 3).reshape(4, 8, 256)
    dpn = jnp.einsum("ihj,ch->ijc", d_local, pair_w.astype(F32))
    d_wb = jnp.einsum("ijc,ihj->hc", pn.astype(F32), d_local)
    d_pg = jnp.sum(unit * dpn, axis=(0, 1))
    g = dpn * pair_gain
    mean = jnp.mean(g, axis=-1, keepdims=True)
    cross = jnp.mean(g * unit, axis=-1, keepdims=True)
    dpair = (inverse * (g - mean - unit * cross)).astype(BF16)

    extra = jnp.concatenate([d_wb, d_pg[None], jnp.zeros((7, 128), F32)], axis=0)
    grad = lax.dynamic_update_slice(grad, extra[None], (0, 1288, 0))
    half = jnp.sum(lax.all_to_all(grad, "core", 0, 0, tiled=True), axis=0)
    parts = lax.all_to_all(half.astype(BF16), AXIAL, 0, 0, tiled=True)
    mine = jnp.sum(parts.reshape(64, ROWS // 64, 128).astype(F32), axis=0)
    mine = mine + lax.ppermute(mine, "x_lo", [(0, 1), (1, 0)])
    total = mine
    for axis in ("x_hi", "z", "y"):
        total = lax.all_gather(total, axis, tiled=True)
    total = lax.all_gather(total, "core")
    f = float(524288) ** (-0.5)
    fp = float(262144) ** (-0.5)
    joined = jnp.concatenate([total[0, :1288], total[1, :1288]], axis=1) * f
    return (
        dx[None],
        dpair[None],
        joined[:1024].T,
        joined[1280],
        joined[1024:1280],
        joined[1281],
        joined[1282],
        total[0, 1296] * fp,
        total[0, 1288:1296].T * fp,
    )


def solution(mesh):
    fine = Mesh(mesh.devices.reshape(2, 2, 4, 8, 2), ("x_lo", "core", "y", "z", "x_hi"))
    split = P(("x_lo", "core"), AXIAL)
    return jax.shard_map(
        local,
        mesh=fine,
        in_specs=(split,) * 3 + (P(),) * 7,
        out_specs=(split, split) + (P(),) * 7,
        check_vma=False,
    )
```

```python
import jax
import jax.numpy as jnp
from jax import lax
from jax.experimental import pallas as pl
from jax.experimental.pallas import tpu as pltpu
from jax.sharding import Mesh, PartitionSpec as P

EPS = 1e-05
F32 = jnp.float32
BF16 = jnp.bfloat16
AXIAL = ("y", "z", "x_hi")
PLANE = ("y", "x_hi")
SENT = [(y * 2 + x) * 8 + z for y in range(4) for z in range(8) for x in range(2)]
TINY = pl.CostEstimate(flops=1000, bytes_accessed=1000, transcendentals=0)
VMEM_LIMIT = 56 * 1024 * 1024

NN = (((1,), (0,)), ((), ()))
NT = (((1,), (1,)), ((), ()))


def mm(a, b, dims=NN):
    return lax.dot_general(a, b, dims, preferred_element_type=F32)


def norm_rows(x):
    average = jnp.mean(x, axis=-1, keepdims=True)
    centered = x - average
    inverse = lax.rsqrt(jnp.mean(centered * centered, axis=-1, keepdims=True) + EPS)
    return centered * inverse, inverse


def project_kernel(
    x_ref, adj_ref, w_ref, wo_ref, gain_ref, shift_ref, gbias_ref, column_ref,
    qt_ref, kt_ref, vt_ref, k_ref, v_ref, gt_ref, dgt_ref, dat_ref, xn_ref, copies_ref, wt_ref, gcol_ref,
):
    @pl.when(pl.program_id(0) == 0)
    def _():
        wt_ref[...] = w_ref[...].astype(F32).T.astype(BF16)
        gcol_ref[...] = jnp.broadcast_to(gbias_ref[...], (128, 256)).T
        for r in range(8):
            for z in range(8):
                copies_ref[r, 32 * z : 32 * z + 32, :] = column_ref[z, 32:64, :]

    unit, _ = norm_rows(x_ref[0].astype(F32))
    xn = (unit * gain_ref[...] + shift_ref[...]).astype(BF16)
    xn_ref[0] = xn
    factor = 32 ** (-0.5)
    qt_ref[0] = (mm(wt_ref[0:256, :], xn, NT) * factor).astype(BF16)
    kt_ref[0] = mm(wt_ref[256:512, :], xn, NT).astype(BF16)
    vt_ref[0] = mm(wt_ref[512:768, :], xn, NT).astype(BF16)
    k_ref[0] = mm(xn, w_ref[:, 256:512]).astype(BF16)
    v_ref[0] = mm(xn, w_ref[:, 512:768]).astype(BF16)
    shifted = jnp.concatenate([gcol_ref[...], gcol_ref[...]], axis=1)
    gate = jax.nn.sigmoid(mm(wt_ref[768:1024, :], xn, NT) + shifted)
    dgated = mm(wo_ref[...], adj_ref[0], NT)
    gt_ref[0] = gate
    dgt_ref[0] = dgated
    dat_ref[0] = (dgated * gate).astype(BF16)


def project(x, adj, w, wo, gain, shift, gbias, column):
    rows = x.shape[0]
    block = pl.BlockSpec((1, 256, 256), lambda s: (s, 0, 0))
    whole = lambda a: pl.BlockSpec(a.shape, lambda s: (0,) * a.ndim)
    small = jax.ShapeDtypeStruct((rows, 256, 256), BF16)
    big = jax.ShapeDtypeStruct((rows, 256, 256), F32)
    return pl.pallas_call(
        project_kernel,
        grid=(rows,),
        in_specs=[block, block, whole(w), whole(wo), whole(gain), whole(shift), whole(gbias), whole(column)],
        out_specs=[block] * 9 + [pl.BlockSpec((8, 256, 128), lambda s: (0, 0, 0))],
        out_shape=[small] * 5 + [big, big, small, small, jax.ShapeDtypeStruct((8, 256, 128), F32)],
        scratch_shapes=[pltpu.VMEM((1024, 256), BF16), pltpu.VMEM((256, 128), F32)],
        compiler_params=pltpu.CompilerParams(vmem_limit_bytes=VMEM_LIMIT),
        cost_estimate=TINY,
        name="project",
    )(x, adj, w, wo, gain, shift, gbias, column)


def attend_kernel(
    heads, first, rows, last,
    bias_ref, qt_ref, kt_ref, vt_ref, k_ref, v_ref, gt_ref, dgt_ref, dat_ref, xn_ref, adj_ref, *refs
):
    if last:
        other_ref, dp_ref, gb_ref, send_ref, bt_ref, acc_ref, out_ref, w_ref, stage_ref = refs
    else:
        dp_ref, gb_ref, send_ref, grad_ref, bt_ref, acc_ref, out_ref, w_ref = refs
    step = pl.program_id(0)
    width = 32 * heads

    @pl.when(step == 0)
    def _():
        for natural, sent in enumerate(SENT):
            out_ref[32 * natural : 32 * natural + 32, :] = bias_ref[32 * sent : 32 * sent + 32, :]
        for h in range(heads):
            for side in range(2):
                part = out_ref[pl.ds(side * heads + h, 256, stride=2 * heads), :]
                bt_ref[h, 128 * side : 128 * side + 128, :] = part.T
        acc_ref[...] = jnp.zeros_like(acc_ref)
        gb_ref[...] = jnp.zeros_like(gb_ref)
        w_ref[...] = jnp.zeros_like(w_ref)

    def own(block, at):
        parts = []
        if at:
            parts.append(jnp.zeros((32 * at, 256), BF16))
        parts.append(block)
        if at < 3:
            parts.append(jnp.zeros((32 * (3 - at), 256), BF16))
        return jnp.concatenate(parts, axis=0)

    gated = [[] for _ in range(2)]

    def place(h):
        head = first + h
        return slice(32 * head, 32 * head + 32), head // 4, head % 4

    def score(r, h):
        here, group, at = place(h)
        lanes = slice(128 * group, 128 * group + 128)
        st = mm(k_ref[r, :, lanes], own(qt_ref[r, here, :], at))
        dpt = mm(v_ref[r, :, lanes], own(dat_ref[r, here, :], at))
        return st, dpt

    def soft(r, h, st, dpt):
        st = st + bt_ref[h]
        e = jnp.exp(st - jnp.max(st, axis=0, keepdims=True))
        p = e * (1.0 / jnp.sum(e, axis=0, keepdims=True))
        delta = jnp.sum(p * dpt, axis=0, keepdims=True)
        ds = p * (dpt - delta)
        acc_ref[h] += ds
        return p.astype(BF16), ds.astype(BF16)

    def half_soft(r, h, st, dpt):
        ps, dss = [], []
        for side in range(2):
            at = slice(128 * side, 128 * side + 128)
            x = st[:, at] + bt_ref[h, :, at]
            e = jnp.exp(x - jnp.max(x, axis=0, keepdims=True))
            p = e * (1.0 / jnp.sum(e, axis=0, keepdims=True))
            d = dpt[:, at]
            delta = jnp.sum(p * d, axis=0, keepdims=True)
            ds = p * (d - delta)
            acc_ref[h, :, at] += ds
            ps.append(p.astype(BF16))
            dss.append(ds.astype(BF16))
        return jnp.concatenate(ps, axis=1), jnp.concatenate(dss, axis=1)

    def close(r, h, p_low, ds_low):
        here, _, _ = place(h)
        out = slice(32 * h, 32 * h + 32)
        att = mm(vt_ref[r, here, :], p_low)
        g = gt_ref[r, here, :]
        graw = dgt_ref[r, here, :] * att * g * (1.0 - g)
        gated[r].append((g * att).astype(BF16))
        gb_ref[out, :] += graw[:, :128] + graw[:, 128:]
        dp_ref[r, 0, out, :] = (mm(kt_ref[r, here, :], ds_low) * (32 ** (-0.5))).astype(BF16)
        dp_ref[r, 1, out, :] = mm(qt_ref[r, here, :], ds_low, NT).astype(BF16)
        dp_ref[r, 2, out, :] = mm(dat_ref[r, here, :], p_low, NT).astype(BF16)
        dp_ref[r, 3, out, :] = graw.astype(BF16)

    items = [(r, h) for r in range(2) for h in range(heads)]
    scores = [score(*items[0])]
    lows = []
    for n, item in enumerate(items):
        if n + 1 < len(items):
            scores.append(score(*items[n + 1]))
        lows.append(half_soft(*item, *scores[n]))
        if n:
            close(*items[n - 1], *lows[n - 1])
    close(*items[-1], *lows[-1])

    xn = xn_ref[...].reshape(256 * 2, 256)
    for b in range(4):
        both = jnp.concatenate([dp_ref[r, b] for r in range(2)], axis=1)
        w_ref[width * b : width * b + width, :] += mm(both, xn)
    both = jnp.concatenate([jnp.concatenate(g, axis=0) for g in gated], axis=1)
    w_ref[4 * width : 5 * width, :] += mm(both, adj_ref[...].reshape(256 * 2, 256))

    @pl.when(step == rows // 2 - 1)
    def _():
        for h in range(heads):
            for side in range(2):
                part = acc_ref[h, 128 * side : 128 * side + 128, :]
                out_ref[pl.ds(side * heads + h, 256, stride=2 * heads), :] = part.T
        if not last:
            for natural, sent in enumerate(SENT):
                send_ref[sent] = out_ref[32 * natural : 32 * natural + 32, :].astype(BF16)
            for side in range(2):
                grad_ref[side] = w_ref[:, 128 * side : 128 * side + 128]
        else:
            for natural, sent in enumerate(SENT):
                stage_ref[sent, 0:32, :] = out_ref[32 * natural : 32 * natural + 32, :]
            for side in range(2):
                for b in range(5):
                    for c in range(2):
                        for r in range(16):
                            g8 = 160 * side + 32 * b + 16 * c + r
                            at = 128 * b + 8 * r
                            if c:
                                piece = w_ref[at : at + 8, 128 * side : 128 * side + 128]
                            else:
                                piece = other_ref[side, at : at + 8, :]
                            to = 32 + 8 * (g8 % 5)
                            stage_ref[g8 // 5, to : to + 8, :] = piece
            send_ref[...] = stage_ref[...].astype(BF16)


def attend(bias, qt, kt, vt, k, v, gt, dgt, dat, xn, adj, first, other):
    rows, heads = qt.shape[0], 4
    last = other is not None
    block = pl.BlockSpec((2, 256, 256), lambda s: (s, 0, 0))
    width = 32 * heads

    def kernel(*refs):
        attend_kernel(heads, first, rows, last, *refs)

    in_specs = [pl.BlockSpec((512 * heads, 128), lambda s: (0, 0))] + [block] * 10
    out_specs = [
        pl.BlockSpec((2, 4, width, 256), lambda s: (s, 0, 0, 0)),
        pl.BlockSpec((width, 128), lambda s: (0, 0)),
    ]
    out_shape = [
        jax.ShapeDtypeStruct((rows, 4, width, 256), BF16),
        jax.ShapeDtypeStruct((width, 128), F32),
    ]
    scratch = [
        pltpu.VMEM((heads, 256, 256), F32),
        pltpu.VMEM((heads, 256, 256), F32),
        pltpu.VMEM((512 * heads, 128), F32),
        pltpu.VMEM((5 * width, 256), F32),
    ]
    operands = [bias, qt, kt, vt, k, v, gt, dgt, dat, xn, adj]
    if last:
        in_specs.append(pl.BlockSpec((2, 5 * width, 128), lambda s: (0, 0, 0)))
        out_specs.append(pl.BlockSpec((64, 72, 128), lambda s: (0, 0, 0)))
        out_shape.append(jax.ShapeDtypeStruct((64, 72, 128), BF16))
        scratch.append(pltpu.VMEM((64, 72, 128), F32))
        operands.append(other)
    else:
        out_specs.append(pl.BlockSpec((64, 8 * heads, 128), lambda s: (0, 0, 0)))
        out_shape.append(jax.ShapeDtypeStruct((64, 8 * heads, 128), BF16))
        out_specs.append(pl.BlockSpec((2, 5 * width, 128), lambda s: (0, 0, 0)))
        out_shape.append(jax.ShapeDtypeStruct((2, 5 * width, 128), F32))
    return pl.pallas_call(
        kernel,
        grid=(rows // 2,),
        in_specs=in_specs,
        out_specs=out_specs,
        out_shape=out_shape,
        scratch_shapes=scratch,
        compiler_params=pltpu.CompilerParams(vmem_limit_bytes=VMEM_LIMIT),
        cost_estimate=TINY,
        name="attend",
    )(*operands)


def inputs_kernel(
    rows, x_ref, w_ref, gain_ref, dpa_ref, dpb_ref, gba_ref, gbb_ref,
    dx_ref, small_ref, mg_ref, mb_ref,
):
    step = pl.program_id(0)

    @pl.when(step == 0)
    def _():
        mg_ref[...] = jnp.zeros_like(mg_ref)
        mb_ref[...] = jnp.zeros_like(mb_ref)

    unit, inverse = norm_rows(x_ref[0].astype(F32))
    gain = gain_ref[...]
    dp = jnp.concatenate([r[0, b] for b in range(4) for r in (dpa_ref, dpb_ref)], axis=0)
    dn = mm(w_ref[...], dp).T
    mg_ref[...] += jnp.sum(unit * dn, axis=0, keepdims=True)
    mb_ref[...] += jnp.sum(dn, axis=0, keepdims=True)
    g = dn * gain
    mean = jnp.mean(g, axis=-1, keepdims=True)
    cross = jnp.mean(g * unit, axis=-1, keepdims=True)
    dx_ref[0] = (inverse * (g - mean - unit * cross)).astype(BF16)

    @pl.when(step == rows - 1)
    def _():
        gb = [jnp.sum(r[...].T, axis=0, keepdims=True) for r in (gba_ref, gbb_ref)]
        mg, mb = mg_ref[...], mb_ref[...]
        small_ref[...] = jnp.concatenate(
            gb + [mg[:, :128], mg[:, 128:], mb[:, :128], mb[:, 128:], jnp.zeros((2, 128), F32)], axis=0
        )


def inputs_grad(x, w, gain, dp_a, dp_b, gb_a, gb_b):
    rows = x.shape[0]
    block = pl.BlockSpec((1, 256, 256), lambda s: (s, 0, 0))
    quad = pl.BlockSpec((1, 4, 128, 256), lambda s: (s, 0, 0, 0))
    whole = lambda a: pl.BlockSpec(a.shape, lambda s: (0,) * a.ndim)

    def kernel(*refs):
        inputs_kernel(rows, *refs)

    return pl.pallas_call(
        kernel,
        grid=(rows,),
        in_specs=[block, whole(w), whole(gain), quad, quad, whole(gb_a), whole(gb_b)],
        out_specs=[block, pl.BlockSpec((8, 128), lambda s: (0, 0))],
        out_shape=[
            jax.ShapeDtypeStruct((rows, 256, 256), BF16),
            jax.ShapeDtypeStruct((8, 128), F32),
        ],
        scratch_shapes=[pltpu.VMEM((1, 256), F32), pltpu.VMEM((1, 256), F32)],
        compiler_params=pltpu.CompilerParams(vmem_limit_bytes=VMEM_LIMIT),
        cost_estimate=TINY,
        name="inputs_grad",
    )(x, w, gain, dp_a, dp_b, gb_a, gb_b)


def unpack_kernel(total_ref, dw_ref, dwo_ref, gb_ref, mg_ref, mb_ref, pg_ref, wb_ref, all_ref, main_ref):
    f = float(524288) ** (-0.5)
    fp = float(262144) ** (-0.5)
    all_ref[...] = total_ref[...].astype(F32)
    for g8 in range(320):
        at = 8 * (g8 % 5)
        main_ref[8 * g8 : 8 * g8 + 8, :] = all_ref[g8 // 5, at : at + 8, :] * f
    for side in range(2):
        lanes = slice(128 * side, 128 * side + 128)
        base = 1280 * side
        dw_ref[lanes, :] = main_ref[base : base + 1024, :].T
        dwo_ref[:, lanes] = main_ref[base + 1024 : base + 1280, :]
    tail = jnp.sum(all_ref[:, 40:56, :], axis=0)
    for n, ref in enumerate((gb_ref, mg_ref, mb_ref)):
        ref[...] = jnp.concatenate([tail[2 * n : 2 * n + 1], tail[2 * n + 1 : 2 * n + 2]], axis=1) * f
    pg_ref[...] = tail[6:7] * fp
    wb_ref[...] = (tail[8:16] * fp).T


def unpack(total):
    vector = jax.ShapeDtypeStruct((1, 256), F32)
    return pl.pallas_call(
        unpack_kernel,
        out_shape=[
            jax.ShapeDtypeStruct((256, 1024), F32),
            jax.ShapeDtypeStruct((256, 256), F32),
            vector, vector, vector,
            jax.ShapeDtypeStruct((1, 128), F32),
            jax.ShapeDtypeStruct((128, 8), F32),
        ],
        scratch_shapes=[pltpu.VMEM((64, 56, 128), F32), pltpu.VMEM((2560, 128), F32)],
        compiler_params=pltpu.CompilerParams(vmem_limit_bytes=VMEM_LIMIT),
        cost_estimate=TINY,
        name="unpack",
    )(total)


def pair_bias_kernel(pair_ref, gain_ref, w_ref, own_ref):
    wt = w_ref[...].astype(F32).T.astype(BF16)
    for i in range(4):
        for side in range(2):
            unit, _ = norm_rows(pair_ref[i, 128 * side : 128 * side + 128, :].astype(F32))
            both = mm(wt, (unit * gain_ref[...]).astype(BF16), NT)
            at = 8 * i + 4 * side
            own_ref[at : at + 4, :] = both[0:4]
            own_ref[32 + at : 36 + at, :] = both[4:8]


def pair_bias(pair, gain, w):
    return pl.pallas_call(
        pair_bias_kernel,
        out_shape=jax.ShapeDtypeStruct((64, 128), F32),
        compiler_params=pltpu.CompilerParams(vmem_limit_bytes=VMEM_LIMIT),
        cost_estimate=TINY,
        name="pair_bias",
    )(pair, gain, w)


def pair_grad_kernel(parts_ref, small_ref, pair_ref, gain_ref, w_ref, dpair_ref, block_ref, mine_ref):
    mine_ref[...] = jnp.sum(parts_ref[...].astype(F32), axis=0)
    wt = w_ref[...].astype(F32).T
    gain = gain_ref[...]
    d_wb = jnp.zeros((8, 128), F32)
    d_pg = jnp.zeros((1, 128), F32)
    high = lax.Precision.HIGHEST
    for i in range(4):
        for side in range(2):
            here = slice(128 * side, 128 * side + 128)
            at = 8 * i + 4 * side
            d_bias = jnp.concatenate([mine_ref[at : at + 4, :], mine_ref[32 + at : 36 + at, :]], axis=0)
            unit, inverse = norm_rows(pair_ref[i, here, :].astype(F32))
            normed = (unit * gain).astype(BF16).astype(F32)
            dpn = lax.dot_general(d_bias.T, wt, NN, precision=high, preferred_element_type=F32)
            d_wb += lax.dot_general(d_bias, normed, NN, precision=high, preferred_element_type=F32)
            d_pg += jnp.sum(unit * dpn, axis=0, keepdims=True)
            g = dpn * gain
            mean = jnp.mean(g, axis=-1, keepdims=True)
            cross = jnp.mean(g * unit, axis=-1, keepdims=True)
            dpair_ref[i, here, :] = (inverse * (g - mean - unit * cross)).astype(BF16)
    block_ref[0:40, :] = mine_ref[64:104, :]
    block_ref[40:48, :] = jnp.concatenate([small_ref[0:6, :], d_pg, small_ref[7:8, :]], axis=0)
    block_ref[48:56, :] = d_wb


def pair_grad(parts, small, pair, gain, w):
    return pl.pallas_call(
        pair_grad_kernel,
        out_shape=[
            jax.ShapeDtypeStruct((4, 256, 128), BF16),
            jax.ShapeDtypeStruct((56, 128), F32),
        ],
        scratch_shapes=[pltpu.VMEM((104, 128), F32)],
        compiler_params=pltpu.CompilerParams(vmem_limit_bytes=VMEM_LIMIT),
        cost_estimate=TINY,
        name="pair_grad",
    )(parts, small, pair, gain, w)


def exchange(blocks, axes):
    return lax.all_to_all(blocks, axes, 0, 0, tiled=True)


def spread(block, count, axes):
    return exchange(jnp.broadcast_to(block[None], (count,) + block.shape), axes)


def local(x, pair, adj, w, gbias, wo, gain, shift, pair_gain, pair_w):
    x, adj, pair = x[0], adj[0], pair[0]
    gain2, shift2 = gain.reshape(1, 256), shift.reshape(1, 256)
    pair_gain2 = pair_gain.reshape(1, 128)
    column = spread(pair_bias(pair, pair_gain2, pair_w), 8, "z")
    bias_a = spread(column[:, :32], 8, PLANE).reshape(2048, 128)
    *made, copies = project(x, adj, w, wo, gain2, shift2, gbias.reshape(1, 256), column)
    bias_b = exchange(copies, PLANE).reshape(2048, 128)

    dp_a, gb_a, send_a, grad_a = attend(bias_a, *made, adj, 0, None)
    dp_b, gb_b, send_b = attend(bias_b, *made, adj, 4, grad_a)
    dx, small = inputs_grad(x, w, gain2, dp_a, dp_b, gb_a, gb_b)

    sums = [
        jnp.sum(exchange(t.reshape(8, 8, -1, 128), PLANE).astype(F32), axis=0).astype(BF16)
        for t in (send_a, send_b)
    ]
    parts = exchange(jnp.concatenate(sums, axis=1), "z")
    dpair, block = pair_grad(parts, small, pair, pair_gain2, pair_w)
    block = block + lax.ppermute(block, "core", [(0, 1), (1, 0)])
    block = block + lax.ppermute(block, "x_lo", [(0, 1), (1, 0)])
    total = spread(spread(block.astype(BF16), 8, "z"), 8, PLANE).reshape(64, 56, 128)
    dw, dwo, gb, mg, mb, pg, wb = unpack(total)
    return (
        dx[None],
        dpair[None],
        dw,
        gb.reshape(256),
        dwo,
        mg.reshape(256),
        mb.reshape(256),
        pg.reshape(128),
        wb,
    )


def solution(mesh):
    fine = Mesh(mesh.devices.reshape(2, 2, 4, 8, 2), ("x_lo", "core", "y", "z", "x_hi"))
    split = P(("x_lo", "core"), AXIAL)
    return jax.shard_map(
        local,
        mesh=fine,
        in_specs=(split,) * 3 + (P(),) * 7,
        out_specs=(split, split) + (P(),) * 7,
        check_vma=False,
    )
```

```python
import jax
import jax.numpy as jnp
from jax import lax
from jax.experimental import pallas as pl
from jax.experimental.pallas import tpu as pltpu
from jax.sharding import Mesh, PartitionSpec as P

EPS = 1e-05
F32 = jnp.float32
BF16 = jnp.bfloat16
AXIAL = ("y", "z", "x_hi")
PLANE = ("y", "x_hi")
SENT = [(y * 2 + x) * 8 + z for y in range(4) for z in range(8) for x in range(2)]
TINY = pl.CostEstimate(flops=1000, bytes_accessed=1000, transcendentals=0)
FIRST = [(side, 8 * n) for side in range(2) for n in range(64)]
SECOND = [(0, side, 8 * n) for side in range(2) for n in range(64, 80)]
SECOND += [(1, side, 8 * n) for side in range(2) for n in range(80)]


def packed_row(chunk, side, row):
    return 1280 * side + 256 * (row // 128) + 128 * chunk + row % 128


GROUPS = [
    [packed_row(0, *g) for g in FIRST[2 * d : 2 * d + 2]] + [packed_row(*g) for g in SECOND[3 * d : 3 * d + 3]]
    for d in range(64)
]
VMEM_LIMIT = 56 * 1024 * 1024

NN = (((1,), (0,)), ((), ()))
NT = (((1,), (1,)), ((), ()))


def mm(a, b, dims=NN):
    return lax.dot_general(a, b, dims, preferred_element_type=F32)


def norm_rows(x):
    average = jnp.mean(x, axis=-1, keepdims=True)
    centered = x - average
    inverse = lax.rsqrt(jnp.mean(centered * centered, axis=-1, keepdims=True) + EPS)
    return centered * inverse, inverse


def project_kernel(
    x_ref, adj_ref, w_ref, wo_ref, gain_ref, shift_ref, gbias_ref, column_ref,
    qt_ref, kt_ref, vt_ref, k_ref, v_ref, gt_ref, dgt_ref, dat_ref, xn_ref, copies_ref, wt_ref, gcol_ref,
):
    @pl.when(pl.program_id(0) == 0)
    def _():
        wt_ref[...] = w_ref[...].astype(F32).T.astype(BF16)
        gcol_ref[...] = jnp.broadcast_to(gbias_ref[...], (128, 256)).T
        for r in range(8):
            for z in range(8):
                copies_ref[r, 32 * z : 32 * z + 32, :] = column_ref[z, 32:64, :]

    unit, _ = norm_rows(x_ref[0].astype(F32))
    xn = (unit * gain_ref[...] + shift_ref[...]).astype(BF16)
    xn_ref[0] = xn
    factor = 32 ** (-0.5)
    qt_ref[0] = (mm(wt_ref[0:256, :], xn, NT) * factor).astype(BF16)
    kt_ref[0] = mm(wt_ref[256:512, :], xn, NT).astype(BF16)
    vt_ref[0] = mm(wt_ref[512:768, :], xn, NT).astype(BF16)
    k_ref[0] = mm(xn, w_ref[:, 256:512]).astype(BF16)
    v_ref[0] = mm(xn, w_ref[:, 512:768]).astype(BF16)
    shifted = jnp.concatenate([gcol_ref[...], gcol_ref[...]], axis=1)
    gate = jax.nn.sigmoid(mm(wt_ref[768:1024, :], xn, NT) + shifted)
    dgated = mm(wo_ref[...], adj_ref[0], NT)
    gt_ref[0] = gate
    dgt_ref[0] = dgated
    dat_ref[0] = (dgated * gate).astype(BF16)


def project(x, adj, w, wo, gain, shift, gbias, column):
    rows = x.shape[0]
    block = pl.BlockSpec((1, 256, 256), lambda s: (s, 0, 0))
    whole = lambda a: pl.BlockSpec(a.shape, lambda s: (0,) * a.ndim)
    small = jax.ShapeDtypeStruct((rows, 256, 256), BF16)
    big = jax.ShapeDtypeStruct((rows, 256, 256), F32)
    return pl.pallas_call(
        project_kernel,
        grid=(rows,),
        in_specs=[block, block, whole(w), whole(wo), whole(gain), whole(shift), whole(gbias), whole(column)],
        out_specs=[block] * 9 + [pl.BlockSpec((8, 256, 128), lambda s: (0, 0, 0))],
        out_shape=[small] * 5 + [big, big, small, small, jax.ShapeDtypeStruct((8, 256, 128), F32)],
        scratch_shapes=[pltpu.VMEM((1024, 256), BF16), pltpu.VMEM((256, 128), F32)],
        compiler_params=pltpu.CompilerParams(vmem_limit_bytes=VMEM_LIMIT),
        cost_estimate=TINY,
        name="project",
    )(x, adj, w, wo, gain, shift, gbias, column)


def attend_kernel(
    heads, first, rows, last,
    bias_ref, qt_ref, kt_ref, vt_ref, k_ref, v_ref, gt_ref, dgt_ref, dat_ref, xn_ref, adj_ref, *refs
):
    if last:
        other_ref, dp_ref, gb_ref, send_ref, bt_ref, acc_ref, out_ref, w_ref, stage_ref = refs
    else:
        dp_ref, gb_ref, send_ref, grad_ref, bt_ref, acc_ref, out_ref, w_ref, stage_ref = refs
    step = pl.program_id(0)
    width = 32 * heads

    @pl.when(step == 0)
    def _():
        for natural, sent in enumerate(SENT):
            out_ref[32 * natural : 32 * natural + 32, :] = bias_ref[32 * sent : 32 * sent + 32, :]
        for h in range(heads):
            for side in range(2):
                part = out_ref[pl.ds(side * heads + h, 256, stride=2 * heads), :]
                bt_ref[h, 128 * side : 128 * side + 128, :] = part.T
        acc_ref[...] = jnp.zeros_like(acc_ref)
        gb_ref[...] = jnp.zeros_like(gb_ref)
        w_ref[...] = jnp.zeros_like(w_ref)

    def own(block, at):
        parts = []
        if at:
            parts.append(jnp.zeros((32 * at, 256), BF16))
        parts.append(block)
        if at < 3:
            parts.append(jnp.zeros((32 * (3 - at), 256), BF16))
        return jnp.concatenate(parts, axis=0)

    gated = [[] for _ in range(2)]

    def place(h):
        head = first + h
        return slice(32 * head, 32 * head + 32), head // 4, head % 4

    def score(r, h):
        here, group, at = place(h)
        lanes = slice(128 * group, 128 * group + 128)
        st = mm(k_ref[r, :, lanes], own(qt_ref[r, here, :], at))
        dpt = mm(v_ref[r, :, lanes], own(dat_ref[r, here, :], at))
        return st, dpt

    def soft(r, h, st, dpt):
        st = st + bt_ref[h]
        e = jnp.exp(st - jnp.max(st, axis=0, keepdims=True))
        p = e * (1.0 / jnp.sum(e, axis=0, keepdims=True))
        delta = jnp.sum(p * dpt, axis=0, keepdims=True)
        ds = p * (dpt - delta)
        acc_ref[h] += ds
        return p.astype(BF16), ds.astype(BF16)

    def half_soft(r, h, st, dpt):
        ps, dss = [], []
        for side in range(2):
            at = slice(128 * side, 128 * side + 128)
            x = st[:, at] + bt_ref[h, :, at]
            e = jnp.exp(x - jnp.max(x, axis=0, keepdims=True))
            p = e * (1.0 / jnp.sum(e, axis=0, keepdims=True))
            d = dpt[:, at]
            delta = jnp.sum(p * d, axis=0, keepdims=True)
            ds = p * (d - delta)
            acc_ref[h, :, at] += ds
            ps.append(p.astype(BF16))
            dss.append(ds.astype(BF16))
        return jnp.concatenate(ps, axis=1), jnp.concatenate(dss, axis=1)

    def close(r, h, p_low, ds_low):
        here, _, _ = place(h)
        out = slice(32 * h, 32 * h + 32)
        att = mm(vt_ref[r, here, :], p_low)
        g = gt_ref[r, here, :]
        graw = dgt_ref[r, here, :] * att * g * (1.0 - g)
        gated[r].append((g * att).astype(BF16))
        gb_ref[out, :] += graw[:, :128] + graw[:, 128:]
        dp_ref[r, 0, out, :] = (mm(kt_ref[r, here, :], ds_low) * (32 ** (-0.5))).astype(BF16)
        dp_ref[r, 1, out, :] = mm(qt_ref[r, here, :], ds_low, NT).astype(BF16)
        dp_ref[r, 2, out, :] = mm(dat_ref[r, here, :], p_low, NT).astype(BF16)
        dp_ref[r, 3, out, :] = graw.astype(BF16)

    items = [(r, h) for r in range(2) for h in range(heads)]
    scores = [score(*items[0])]
    lows = []
    for n, item in enumerate(items):
        if n + 1 < len(items):
            scores.append(score(*items[n + 1]))
        lows.append(half_soft(*item, *scores[n]))
        if n:
            close(*items[n - 1], *lows[n - 1])
    close(*items[-1], *lows[-1])

    xn = xn_ref[...].reshape(256 * 2, 256)
    for b in range(4):
        both = jnp.concatenate([dp_ref[r, b] for r in range(2)], axis=1)
        w_ref[width * b : width * b + width, :] += mm(both, xn)
    both = jnp.concatenate([jnp.concatenate(g, axis=0) for g in gated], axis=1)
    w_ref[4 * width : 5 * width, :] += mm(both, adj_ref[...].reshape(256 * 2, 256))

    @pl.when(step == rows // 2 - 1)
    def _():
        for h in range(heads):
            for side in range(2):
                part = acc_ref[h, 128 * side : 128 * side + 128, :]
                out_ref[pl.ds(side * heads + h, 256, stride=2 * heads), :] = part.T
        for natural, sent in enumerate(SENT):
            stage_ref[sent, 0:32, :] = out_ref[32 * natural : 32 * natural + 32, :]
        if not last:
            for n, (side, row) in enumerate(FIRST):
                to = 32 + 8 * (n % 2)
                stage_ref[n // 2, to : to + 8, :] = w_ref[row : row + 8, 128 * side : 128 * side + 128]
            for side in range(2):
                grad_ref[side] = w_ref[512:640, 128 * side : 128 * side + 128]
        else:
            for n, (c, side, row) in enumerate(SECOND):
                to = 32 + 8 * (n % 3)
                if c:
                    piece = w_ref[row : row + 8, 128 * side : 128 * side + 128]
                else:
                    piece = other_ref[side, row - 512 : row - 504, :]
                stage_ref[n // 3, to : to + 8, :] = piece
        send_ref[...] = stage_ref[...].astype(BF16)


def attend(bias, qt, kt, vt, k, v, gt, dgt, dat, xn, adj, first, other):
    rows, heads = qt.shape[0], 4
    last = other is not None
    block = pl.BlockSpec((2, 256, 256), lambda s: (s, 0, 0))
    width = 32 * heads

    def kernel(*refs):
        attend_kernel(heads, first, rows, last, *refs)

    in_specs = [pl.BlockSpec((512 * heads, 128), lambda s: (0, 0))] + [block] * 10
    out_specs = [
        pl.BlockSpec((2, 4, width, 256), lambda s: (s, 0, 0, 0)),
        pl.BlockSpec((width, 128), lambda s: (0, 0)),
    ]
    out_shape = [
        jax.ShapeDtypeStruct((rows, 4, width, 256), BF16),
        jax.ShapeDtypeStruct((width, 128), F32),
    ]
    scratch = [
        pltpu.VMEM((heads, 256, 256), F32),
        pltpu.VMEM((heads, 256, 256), F32),
        pltpu.VMEM((512 * heads, 128), F32),
        pltpu.VMEM((5 * width, 256), F32),
    ]
    operands = [bias, qt, kt, vt, k, v, gt, dgt, dat, xn, adj]
    height = 8 * heads + (24 if last else 16)
    out_specs.append(pl.BlockSpec((64, height, 128), lambda s: (0, 0, 0)))
    out_shape.append(jax.ShapeDtypeStruct((64, height, 128), BF16))
    scratch.append(pltpu.VMEM((64, height, 128), F32))
    rest = pl.BlockSpec((2, width, 128), lambda s: (0, 0, 0))
    if last:
        in_specs.append(rest)
        operands.append(other)
    else:
        out_specs.append(rest)
        out_shape.append(jax.ShapeDtypeStruct((2, width, 128), F32))
    return pl.pallas_call(
        kernel,
        grid=(rows // 2,),
        in_specs=in_specs,
        out_specs=out_specs,
        out_shape=out_shape,
        scratch_shapes=scratch,
        compiler_params=pltpu.CompilerParams(vmem_limit_bytes=VMEM_LIMIT),
        cost_estimate=TINY,
        name="attend",
    )(*operands)


def inputs_kernel(
    rows, x_ref, w_ref, gain_ref, dpa_ref, dpb_ref, gba_ref, gbb_ref,
    dx_ref, small_ref, mg_ref, mb_ref,
):
    step = pl.program_id(0)

    @pl.when(step == 0)
    def _():
        mg_ref[...] = jnp.zeros_like(mg_ref)
        mb_ref[...] = jnp.zeros_like(mb_ref)

    unit, inverse = norm_rows(x_ref[0].astype(F32))
    gain = gain_ref[...]
    dp = jnp.concatenate([r[0, b] for b in range(4) for r in (dpa_ref, dpb_ref)], axis=0)
    dn = mm(w_ref[...], dp).T
    mg_ref[...] += jnp.sum(unit * dn, axis=0, keepdims=True)
    mb_ref[...] += jnp.sum(dn, axis=0, keepdims=True)
    g = dn * gain
    mean = jnp.mean(g, axis=-1, keepdims=True)
    cross = jnp.mean(g * unit, axis=-1, keepdims=True)
    dx_ref[0] = (inverse * (g - mean - unit * cross)).astype(BF16)

    @pl.when(step == rows - 1)
    def _():
        gb = [jnp.sum(r[...].T, axis=0, keepdims=True) for r in (gba_ref, gbb_ref)]
        mg, mb = mg_ref[...], mb_ref[...]
        small_ref[...] = jnp.concatenate(
            gb + [mg[:, :128], mg[:, 128:], mb[:, :128], mb[:, 128:], jnp.zeros((2, 128), F32)], axis=0
        )


def inputs_grad(x, w, gain, dp_a, dp_b, gb_a, gb_b):
    rows = x.shape[0]
    block = pl.BlockSpec((1, 256, 256), lambda s: (s, 0, 0))
    quad = pl.BlockSpec((1, 4, 128, 256), lambda s: (s, 0, 0, 0))
    whole = lambda a: pl.BlockSpec(a.shape, lambda s: (0,) * a.ndim)

    def kernel(*refs):
        inputs_kernel(rows, *refs)

    return pl.pallas_call(
        kernel,
        grid=(rows,),
        in_specs=[block, whole(w), whole(gain), quad, quad, whole(gb_a), whole(gb_b)],
        out_specs=[block, pl.BlockSpec((8, 128), lambda s: (0, 0))],
        out_shape=[
            jax.ShapeDtypeStruct((rows, 256, 256), BF16),
            jax.ShapeDtypeStruct((8, 128), F32),
        ],
        scratch_shapes=[pltpu.VMEM((1, 256), F32), pltpu.VMEM((1, 256), F32)],
        compiler_params=pltpu.CompilerParams(vmem_limit_bytes=VMEM_LIMIT),
        cost_estimate=TINY,
        name="inputs_grad",
    )(x, w, gain, dp_a, dp_b, gb_a, gb_b)


def unpack_kernel(total_ref, dw_ref, dwo_ref, gb_ref, mg_ref, mb_ref, pg_ref, wb_ref, all_ref, main_ref):
    f = float(524288) ** (-0.5)
    fp = float(262144) ** (-0.5)
    all_ref[...] = total_ref[...].astype(F32)
    for d in range(64):
        for k, row in enumerate(GROUPS[d]):
            at = 40 * (d % 8) + 8 * k
            main_ref[row : row + 8, :] = all_ref[d // 8, at : at + 8, :] * f
    for side in range(2):
        lanes = slice(128 * side, 128 * side + 128)
        base = 1280 * side
        dw_ref[lanes, :] = main_ref[base : base + 1024, :].T
        dwo_ref[:, lanes] = main_ref[base + 1024 : base + 1280, :]
    tail = jnp.sum(all_ref[:, 320:336, :], axis=0)
    for n, ref in enumerate((gb_ref, mg_ref, mb_ref)):
        ref[...] = jnp.concatenate([tail[2 * n : 2 * n + 1], tail[2 * n + 1 : 2 * n + 2]], axis=1) * f
    pg_ref[...] = tail[6:7] * fp
    wb_ref[...] = tail[8:16] * fp


def unpack(total):
    vector = jax.ShapeDtypeStruct((1, 256), F32)
    return pl.pallas_call(
        unpack_kernel,
        out_shape=[
            jax.ShapeDtypeStruct((256, 1024), F32),
            jax.ShapeDtypeStruct((256, 256), F32),
            vector, vector, vector,
            jax.ShapeDtypeStruct((1, 128), F32),
            jax.ShapeDtypeStruct((8, 128), F32),
        ],
        scratch_shapes=[pltpu.VMEM((8, 336, 128), F32), pltpu.VMEM((2560, 128), F32)],
        compiler_params=pltpu.CompilerParams(vmem_limit_bytes=VMEM_LIMIT),
        cost_estimate=TINY,
        name="unpack",
    )(total)


def pair_bias_kernel(pair_ref, gain_ref, wt_ref, own_ref):
    wt = wt_ref[...]
    for i in range(4):
        for side in range(2):
            unit, _ = norm_rows(pair_ref[i, 128 * side : 128 * side + 128, :].astype(F32))
            both = mm(wt, (unit * gain_ref[...]).astype(BF16), NT)
            at = 8 * i + 4 * side
            for r in range(8):
                own_ref[r, at : at + 4, :] = both[0:4]
                own_ref[r, 32 + at : 36 + at, :] = both[4:8]


def pair_bias(pair, gain, wt):
    return pl.pallas_call(
        pair_bias_kernel,
        out_shape=jax.ShapeDtypeStruct((8, 64, 128), F32),
        compiler_params=pltpu.CompilerParams(vmem_limit_bytes=VMEM_LIMIT),
        cost_estimate=TINY,
        name="pair_bias",
    )(pair, gain, wt)


def pair_grad_kernel(parts_ref, small_ref, pair_ref, gain_ref, wt_ref, dpair_ref, block_ref, mine_ref):
    mine_ref[...] = jnp.sum(parts_ref[...].astype(F32), axis=0)
    wt = jnp.concatenate([wt_ref[...].astype(F32)] * 2, axis=0).astype(BF16)
    gain = gain_ref[...]
    d_wb = jnp.zeros((8, 128), F32)
    d_pg = jnp.zeros((1, 128), F32)
    for i in range(4):
        for side in range(2):
            here = slice(128 * side, 128 * side + 128)
            at = 8 * i + 4 * side
            d_bias = jnp.concatenate([mine_ref[at : at + 4, :], mine_ref[32 + at : 36 + at, :]], axis=0)
            high = d_bias.astype(BF16).astype(F32)
            pieces = jnp.concatenate([high, d_bias - high], axis=0)
            unit, inverse = norm_rows(pair_ref[i, here, :].astype(F32))
            normed = (unit * gain).astype(BF16)
            dpn = mm(pieces.T.astype(BF16), wt)
            both = mm(pieces.astype(BF16), normed)
            d_wb += both[0:8] + both[8:16]
            d_pg += jnp.sum(unit * dpn, axis=0, keepdims=True)
            g = dpn * gain
            mean = jnp.mean(g, axis=-1, keepdims=True)
            cross = jnp.mean(g * unit, axis=-1, keepdims=True)
            dpair_ref[i, here, :] = (inverse * (g - mean - unit * cross)).astype(BF16)
    block_ref[0:40, :] = mine_ref[64:104, :]
    block_ref[40:48, :] = jnp.concatenate([small_ref[0:6, :], d_pg, small_ref[7:8, :]], axis=0)
    block_ref[48:56, :] = d_wb


def pair_grad(parts, small, pair, gain, wt):
    return pl.pallas_call(
        pair_grad_kernel,
        out_shape=[
            jax.ShapeDtypeStruct((4, 256, 128), BF16),
            jax.ShapeDtypeStruct((56, 128), F32),
        ],
        scratch_shapes=[pltpu.VMEM((104, 128), F32)],
        compiler_params=pltpu.CompilerParams(vmem_limit_bytes=VMEM_LIMIT),
        cost_estimate=TINY,
        name="pair_grad",
    )(parts, small, pair, gain, wt)


def exchange(blocks, axes):
    return lax.all_to_all(blocks, axes, 0, 0, tiled=True)


def spread(block, count, axes):
    return exchange(jnp.broadcast_to(block[None], (count,) + block.shape), axes)


def local(x, pair, adj, w, gbias, wo, gain, shift, pair_gain, pair_w):
    x, adj, pair = x[0], adj[0], pair[0]
    gain2, shift2 = gain.reshape(1, 256), shift.reshape(1, 256)
    pair_gain2 = pair_gain.reshape(1, 128)
    pair_wt = pair_w.T
    column = exchange(pair_bias(pair, pair_gain2, pair_wt), "z")
    bias_a = spread(column[:, :32], 8, PLANE).reshape(2048, 128)
    *made, copies = project(x, adj, w, wo, gain2, shift2, gbias.reshape(1, 256), column)
    bias_b = exchange(copies, PLANE).reshape(2048, 128)

    dp_a, gb_a, send_a, grad_a = attend(bias_a, *made, adj, 0, None)
    dp_b, gb_b, send_b = attend(bias_b, *made, adj, 4, grad_a)
    dx, small = inputs_grad(x, w, gain2, dp_a, dp_b, gb_a, gb_b)

    sums = [
        jnp.sum(exchange(t.reshape(8, 8, -1, 128), PLANE).astype(F32), axis=0).astype(BF16)
        for t in (send_a, send_b)
    ]
    order = [sums[0][:, :32], sums[1][:, :32], sums[0][:, 32:], sums[1][:, 32:]]
    parts = exchange(jnp.concatenate(order, axis=1), "z")
    dpair, block = pair_grad(parts, small, pair, pair_gain2, pair_wt)
    others = [
        lax.ppermute(block, ("x_lo", "core"), [(n, n ^ flip) for n in range(4)]) for flip in (1, 2, 3)
    ]
    block = (block + others[0]) + (others[1] + others[2])
    line = spread(block.astype(BF16), 8, "z")
    tail = jnp.sum(line[:, 40:].astype(F32), axis=0).astype(BF16)
    total = spread(jnp.concatenate([line[:, :40].reshape(320, 128), tail], axis=0), 8, PLANE)
    dw, dwo, gb, mg, mb, pg, wb = unpack(total)
    return (
        dx[None],
        dpair[None],
        dw,
        gb.reshape(256),
        dwo,
        mg.reshape(256),
        mb.reshape(256),
        pg.reshape(128),
        wb.T,
    )


def solution(mesh):
    fine = Mesh(mesh.devices.reshape(2, 2, 4, 8, 2), ("x_lo", "core", "y", "z", "x_hi"))
    split = P(("x_lo", "core"), AXIAL)
    return jax.shard_map(
        local,
        mesh=fine,
        in_specs=(split,) * 3 + (P(),) * 7,
        out_specs=(split, split) + (P(),) * 7,
        check_vma=False,
    )
```

```python
import jax
import jax.numpy as jnp
from jax import lax
from jax.experimental import pallas as pl
from jax.experimental.pallas import tpu as pltpu
from jax.sharding import Mesh, PartitionSpec as P

EPS = 1e-05
F32 = jnp.float32
BF16 = jnp.bfloat16
AXIAL = ("y", "z", "x_hi")
BIAS_INNER, BIAS_OUTER = ("z",), ("y", "x_hi")
GRAD_INNER, GRAD_OUTER = ("z", "x_hi"), ("y",)
BACK_INNER, BACK_OUTER = ("z",), ("y", "x_hi")
SIZES = {"y": 4, "z": 8, "x_hi": 2}


def count(axes):
    total = 1
    for axis in axes:
        total *= SIZES[axis]
    return total


def places(outer, inner):
    result = []
    for y in range(4):
        for z in range(8):
            for x in range(2):
                place = 0
                for axis in outer + inner:
                    place = place * SIZES[axis] + {"y": y, "z": z, "x_hi": x}[axis]
                result.append(place)
    return result


BIAS_SENT = places(BIAS_OUTER, BIAS_INNER)
GRAD_SENT = places(GRAD_OUTER, GRAD_INNER)
BACK_SENT = places(BACK_OUTER, BACK_INNER)
BI, BO, GI, GO = (count(axes) for axes in (BIAS_INNER, BIAS_OUTER, GRAD_INNER, GRAD_OUTER))
RI, RO = count(BACK_INNER), count(BACK_OUTER)
TINY = pl.CostEstimate(flops=1000, bytes_accessed=1000, transcendentals=0)
FIRST = [(side, 8 * n) for side in range(2) for n in range(64)]
SECOND = [(0, side, 8 * n) for side in range(2) for n in range(64, 80)]
SECOND += [(1, side, 8 * n) for side in range(2) for n in range(80)]


def packed_row(chunk, side, row):
    return 1280 * side + 256 * (row // 128) + 128 * chunk + row % 128


GROUPS = [
    [packed_row(0, *g) for g in FIRST[2 * d : 2 * d + 2]] + [packed_row(*g) for g in SECOND[3 * d : 3 * d + 3]]
    for d in range(64)
]
MIB = 1024 * 1024

NN = (((1,), (0,)), ((), ()))
NT = (((1,), (1,)), ((), ()))


def mm(a, b, dims=NN):
    return lax.dot_general(a, b, dims, preferred_element_type=F32)


def norm_rows(x):
    average = jnp.mean(x, axis=-1, keepdims=True)
    centered = x - average
    inverse = lax.rsqrt(jnp.mean(centered * centered, axis=-1, keepdims=True) + EPS)
    return centered * inverse, inverse


def project_kernel(
    x_ref, adj_ref, w_ref, wo_ref, gain_ref, shift_ref, gbias_ref, column_ref,
    qt_ref, kt_ref, vt_ref, k_ref, v_ref, gt_ref, dgt_ref, dat_ref, xn_ref, copies_ref, wt_ref, gcol_ref,
):
    @pl.when(pl.program_id(0) == 0)
    def _():
        wt_ref[...] = w_ref[...].astype(F32).T.astype(BF16)
        gcol_ref[...] = jnp.broadcast_to(gbias_ref[...], (128, 256)).T
        for r in range(BO):
            for z in range(BI):
                copies_ref[r, 32 * z : 32 * z + 32, :] = column_ref[z, 32:64, :]

    unit, _ = norm_rows(x_ref[...].reshape(512, 256).astype(F32))
    xn = (unit * gain_ref[...] + shift_ref[...]).astype(BF16)
    xn_ref[...] = xn.reshape(2, 256, 256)
    k_ref[...] = mm(xn, w_ref[:, 256:512]).astype(BF16).reshape(2, 256, 256)
    v_ref[...] = mm(xn, w_ref[:, 512:768]).astype(BF16).reshape(2, 256, 256)
    factor = 32 ** (-0.5)
    shifted = jnp.concatenate([gcol_ref[...], gcol_ref[...]], axis=1)
    for r in range(2):
        row = xn[256 * r : 256 * r + 256]
        qt_ref[r] = (mm(wt_ref[0:256, :], row, NT) * factor).astype(BF16)
        kt_ref[r] = mm(wt_ref[256:512, :], row, NT).astype(BF16)
        vt_ref[r] = mm(wt_ref[512:768, :], row, NT).astype(BF16)
        gate = jax.nn.sigmoid(mm(wt_ref[768:1024, :], row, NT) + shifted)
        dgated = mm(wo_ref[...], adj_ref[r], NT)
        gt_ref[r] = gate
        dgt_ref[r] = dgated
        dat_ref[r] = (dgated * gate).astype(BF16)


def project(x, adj, w, wo, gain, shift, gbias, column):
    rows = x.shape[0]
    block = pl.BlockSpec((2, 256, 256), lambda s: (s, 0, 0))
    whole = lambda a: pl.BlockSpec(a.shape, lambda s: (0,) * a.ndim)
    small = jax.ShapeDtypeStruct((rows, 256, 256), BF16)
    big = jax.ShapeDtypeStruct((rows, 256, 256), F32)
    return pl.pallas_call(
        project_kernel,
        grid=(rows // 2,),
        in_specs=[block, block, whole(w), whole(wo), whole(gain), whole(shift), whole(gbias), whole(column)],
        out_specs=[block] * 9 + [pl.BlockSpec((BO, 32 * BI, 128), lambda s: (0, 0, 0))],
        out_shape=[small] * 5 + [big, big, small, small, jax.ShapeDtypeStruct((BO, 32 * BI, 128), F32)],
        scratch_shapes=[pltpu.VMEM((1024, 256), BF16), pltpu.VMEM((256, 128), F32)],
        compiler_params=pltpu.CompilerParams(vmem_limit_bytes=56 * MIB),
        cost_estimate=TINY,
        name="project",
    )(x, adj, w, wo, gain, shift, gbias, column)


def attend_kernel(
    heads, rows, last,
    bias_ref, qt_ref, kt_ref, vt_ref, k_ref, v_ref, gt_ref, dgt_ref, dat_ref, xn_ref, adj_ref, *refs
):
    if last:
        other_ref, dp_ref, gb_ref, send_ref, bt_ref, acc_ref, out_ref, w_ref, stage_ref = refs
    else:
        dp_ref, gb_ref, send_ref, grad_ref, bt_ref, acc_ref, out_ref, w_ref, stage_ref = refs
    step = pl.program_id(0)
    width = 32 * heads

    @pl.when(step == 0)
    def _():
        for natural, sent in enumerate(BIAS_SENT):
            out_ref[32 * natural : 32 * natural + 32, :] = bias_ref[32 * sent : 32 * sent + 32, :]
        for h in range(heads):
            for side in range(2):
                part = out_ref[pl.ds(side * heads + h, 256, stride=2 * heads), :]
                bt_ref[h, 128 * side : 128 * side + 128, :] = part.T
        acc_ref[...] = jnp.zeros_like(acc_ref)
        gb_ref[...] = jnp.zeros_like(gb_ref)
        w_ref[...] = jnp.zeros_like(w_ref)

    def own(block, at):
        parts = []
        if at:
            parts.append(jnp.zeros((32 * at, 256), BF16))
        parts.append(block)
        if at < 3:
            parts.append(jnp.zeros((32 * (3 - at), 256), BF16))
        return jnp.concatenate(parts, axis=0)

    gated = [[] for _ in range(2)]

    def place(h):
        return slice(32 * h, 32 * h + 32)

    def score(r, h):
        here = place(h)
        st = mm(k_ref[r], own(qt_ref[r, here, :], h))
        dpt = mm(v_ref[r], own(dat_ref[r, here, :], h))
        return st, dpt

    def soft(r, h, st, dpt):
        st = st + bt_ref[h]
        e = jnp.exp(st - jnp.max(st, axis=0, keepdims=True))
        p = e * (1.0 / jnp.sum(e, axis=0, keepdims=True))
        delta = jnp.sum(p * dpt, axis=0, keepdims=True)
        ds = p * (dpt - delta)
        acc_ref[h] += ds
        return p.astype(BF16), ds.astype(BF16)

    def half_soft(r, h, st, dpt):
        ps, dss = [], []
        for side in range(2):
            at = slice(128 * side, 128 * side + 128)
            x = st[:, at] + bt_ref[h, :, at]
            e = jnp.exp(x - jnp.max(x, axis=0, keepdims=True))
            p = e * (1.0 / jnp.sum(e, axis=0, keepdims=True))
            d = dpt[:, at]
            delta = jnp.sum(p * d, axis=0, keepdims=True)
            ds = p * (d - delta)
            acc_ref[h, :, at] += ds
            ps.append(p.astype(BF16))
            dss.append(ds.astype(BF16))
        return jnp.concatenate(ps, axis=1), jnp.concatenate(dss, axis=1)

    def close(r, h, p_low, ds_low):
        here = place(h)
        out = slice(32 * h, 32 * h + 32)
        att = mm(vt_ref[r, here, :], p_low)
        g = gt_ref[r, here, :]
        graw = dgt_ref[r, here, :] * att * g * (1.0 - g)
        gated[r].append((g * att).astype(BF16))
        gb_ref[out, :] += graw[:, :128] + graw[:, 128:]
        dp_ref[r, 0, out, :] = (mm(kt_ref[r, here, :], ds_low) * (32 ** (-0.5))).astype(BF16)
        dp_ref[r, 1, out, :] = mm(qt_ref[r, here, :], ds_low, NT).astype(BF16)
        dp_ref[r, 2, out, :] = mm(dat_ref[r, here, :], p_low, NT).astype(BF16)
        dp_ref[r, 3, out, :] = graw.astype(BF16)

    items = [(r, h) for r in range(2) for h in range(heads)]
    scores = [score(*items[0])]
    lows = []
    for n, item in enumerate(items):
        if n + 1 < len(items):
            scores.append(score(*items[n + 1]))
        lows.append(half_soft(*item, *scores[n]))
        if n:
            close(*items[n - 1], *lows[n - 1])
    close(*items[-1], *lows[-1])

    xn = xn_ref[...].reshape(256 * 2, 256)
    for b in range(4):
        both = jnp.concatenate([dp_ref[r, b] for r in range(2)], axis=1)
        w_ref[width * b : width * b + width, :] += mm(both, xn)
    both = jnp.concatenate([jnp.concatenate(g, axis=0) for g in gated], axis=1)
    w_ref[4 * width : 5 * width, :] += mm(both, adj_ref[...].reshape(256 * 2, 256))

    @pl.when(step == rows // 2 - 1)
    def _():
        for h in range(heads):
            for side in range(2):
                part = acc_ref[h, 128 * side : 128 * side + 128, :]
                out_ref[pl.ds(side * heads + h, 256, stride=2 * heads), :] = part.T
        for natural, sent in enumerate(GRAD_SENT):
            stage_ref[sent, 0:32, :] = out_ref[32 * natural : 32 * natural + 32, :]
        if not last:
            for n, (side, row) in enumerate(FIRST):
                to = 32 + 8 * (n % 2)
                stage_ref[n // 2, to : to + 8, :] = w_ref[row : row + 8, 128 * side : 128 * side + 128]
            for side in range(2):
                grad_ref[side] = w_ref[512:640, 128 * side : 128 * side + 128]
        else:
            for n, (c, side, row) in enumerate(SECOND):
                to = 32 + 8 * (n % 3)
                if c:
                    piece = w_ref[row : row + 8, 128 * side : 128 * side + 128]
                else:
                    piece = other_ref[side, row - 512 : row - 504, :]
                stage_ref[n // 3, to : to + 8, :] = piece
        send_ref[...] = stage_ref[...].astype(BF16)


def attend(bias, qt, kt, vt, k, v, gt, dgt, dat, xn, adj, chunk, other):
    rows, heads = qt.shape[0], 4
    last = other is not None
    block = pl.BlockSpec((2, 256, 256), lambda s: (s, 0, 0))
    width = 32 * heads

    def kernel(*refs):
        attend_kernel(heads, rows, last, *refs)

    half = pl.BlockSpec((2, width, 256), lambda s: (s, chunk, 0))
    columns = pl.BlockSpec((2, 256, width), lambda s: (s, 0, chunk))
    in_specs = [pl.BlockSpec((512 * heads, 128), lambda s: (0, 0))]
    in_specs += [half, half, half, columns, columns, half, half, half, block, block]
    out_specs = [
        pl.BlockSpec((2, 4, width, 256), lambda s: (s, 0, 0, 0)),
        pl.BlockSpec((width, 128), lambda s: (0, 0)),
    ]
    out_shape = [
        jax.ShapeDtypeStruct((rows, 4, width, 256), BF16),
        jax.ShapeDtypeStruct((width, 128), F32),
    ]
    scratch = [
        pltpu.VMEM((heads, 256, 256), F32),
        pltpu.VMEM((heads, 256, 256), F32),
        pltpu.VMEM((512 * heads, 128), F32),
        pltpu.VMEM((5 * width, 256), F32),
    ]
    operands = [bias, qt, kt, vt, k, v, gt, dgt, dat, xn, adj]
    height = 8 * heads + (24 if last else 16)
    out_specs.append(pl.BlockSpec((64, height, 128), lambda s: (0, 0, 0)))
    out_shape.append(jax.ShapeDtypeStruct((64, height, 128), BF16))
    scratch.append(pltpu.VMEM((64, height, 128), F32))
    rest = pl.BlockSpec((2, width, 128), lambda s: (0, 0, 0))
    if last:
        in_specs.append(rest)
        operands.append(other)
    else:
        out_specs.append(rest)
        out_shape.append(jax.ShapeDtypeStruct((2, width, 128), F32))
    return pl.pallas_call(
        kernel,
        grid=(rows // 2,),
        in_specs=in_specs,
        out_specs=out_specs,
        out_shape=out_shape,
        scratch_shapes=scratch,
        compiler_params=pltpu.CompilerParams(vmem_limit_bytes=56 * MIB),
        cost_estimate=TINY,
        name="attend",
    )(*operands)


def inputs_kernel(
    rows, x_ref, w_ref, gain_ref, dpa_ref, dpb_ref, gba_ref, gbb_ref, pair_ref, pgain_ref,
    dx_ref, small_ref, normed_ref, mg_ref, mb_ref,
):
    step = pl.program_id(0)

    @pl.when(step == 0)
    def _():
        mg_ref[...] = jnp.zeros_like(mg_ref)
        mb_ref[...] = jnp.zeros_like(mb_ref)

    pair_unit, _ = norm_rows(pair_ref[0].astype(F32))
    high = pair_unit.astype(BF16)
    normed_ref[:, 0:128] = (pair_unit * pgain_ref[...]).astype(BF16)
    normed_ref[:, 128:256] = high
    normed_ref[:, 256:384] = (pair_unit - high.astype(F32)).astype(BF16)

    unit, inverse = norm_rows(x_ref[0].astype(F32))
    gain = gain_ref[...]
    dp = jnp.concatenate([r[0, b] for b in range(4) for r in (dpa_ref, dpb_ref)], axis=0)
    dn = mm(w_ref[...], dp).T
    mg_ref[...] += jnp.sum(unit * dn, axis=0, keepdims=True)
    mb_ref[...] += jnp.sum(dn, axis=0, keepdims=True)
    g = dn * gain
    mean = jnp.mean(g, axis=-1, keepdims=True)
    cross = jnp.mean(g * unit, axis=-1, keepdims=True)
    dx_ref[0] = (inverse * (g - mean - unit * cross)).astype(BF16)

    @pl.when(step == rows - 1)
    def _():
        gb = [jnp.sum(r[...].T, axis=0, keepdims=True) for r in (gba_ref, gbb_ref)]
        mg, mb = mg_ref[...], mb_ref[...]
        small_ref[...] = jnp.concatenate(
            gb + [mg[:, :128], mg[:, 128:], mb[:, :128], mb[:, 128:], jnp.zeros((2, 128), F32)], axis=0
        )


def inputs_grad(x, w, gain, dp_a, dp_b, gb_a, gb_b, pair, pair_gain):
    rows = x.shape[0]
    block = pl.BlockSpec((1, 256, 256), lambda s: (s, 0, 0))
    quad = pl.BlockSpec((1, 4, 128, 256), lambda s: (s, 0, 0, 0))
    whole = lambda a: pl.BlockSpec(a.shape, lambda s: (0,) * a.ndim)

    def kernel(*refs):
        inputs_kernel(rows, *refs)

    return pl.pallas_call(
        kernel,
        grid=(rows,),
        in_specs=[
            block, whole(w), whole(gain), quad, quad, whole(gb_a), whole(gb_b),
            pl.BlockSpec((1, 128, 128), lambda s: (s // 2, s % 2, 0)), whole(pair_gain),
        ],
        out_specs=[
            block,
            pl.BlockSpec((8, 128), lambda s: (0, 0)),
            pl.BlockSpec((128, 384), lambda s: (s, 0)),
        ],
        out_shape=[
            jax.ShapeDtypeStruct((rows, 256, 256), BF16),
            jax.ShapeDtypeStruct((8, 128), F32),
            jax.ShapeDtypeStruct((1024, 384), BF16),
        ],
        scratch_shapes=[pltpu.VMEM((1, 256), F32), pltpu.VMEM((1, 256), F32)],
        compiler_params=pltpu.CompilerParams(vmem_limit_bytes=56 * MIB),
        cost_estimate=TINY,
        name="inputs_grad",
    )(x, w, gain, dp_a, dp_b, gb_a, gb_b, pair, pair_gain)


def unpack_kernel(total_ref, dw_ref, dwo_ref, gb_ref, mg_ref, mb_ref, pg_ref, wb_ref, all_ref, main_ref):
    f = float(524288) ** (-0.5)
    fp = float(262144) ** (-0.5)
    all_ref[...] = total_ref[...].astype(F32)
    for sent, back in zip(GRAD_SENT, BACK_SENT):
        for k, row in enumerate(GROUPS[sent]):
            at = 40 * (back % RI) + 8 * k
            main_ref[row : row + 8, :] = all_ref[back // RI, at : at + 8, :] * f
    for side in range(2):
        lanes = slice(128 * side, 128 * side + 128)
        base = 1280 * side
        dw_ref[lanes, :] = main_ref[base : base + 1024, :].T
        dwo_ref[:, lanes] = main_ref[base + 1024 : base + 1280, :]
    tail = jnp.sum(all_ref[:, 40 * RI :, :], axis=0)
    for n, ref in enumerate((gb_ref, mg_ref, mb_ref)):
        ref[...] = jnp.concatenate([tail[2 * n : 2 * n + 1], tail[2 * n + 1 : 2 * n + 2]], axis=1) * f
    pg_ref[...] = tail[6:7] * fp
    wb_ref[...] = tail[8:16] * fp


def unpack(total):
    vector = jax.ShapeDtypeStruct((1, 256), F32)
    return pl.pallas_call(
        unpack_kernel,
        out_shape=[
            jax.ShapeDtypeStruct((256, 1024), F32),
            jax.ShapeDtypeStruct((256, 256), F32),
            vector, vector, vector,
            jax.ShapeDtypeStruct((1, 128), F32),
            jax.ShapeDtypeStruct((8, 128), F32),
        ],
        scratch_shapes=[pltpu.VMEM((RO, 40 * RI + 16, 128), F32), pltpu.VMEM((2560, 128), F32)],
        compiler_params=pltpu.CompilerParams(vmem_limit_bytes=12 * MIB),
        cost_estimate=TINY,
        name="unpack",
    )(total)


def pair_bias_kernel(pair_ref, gain_ref, wt_ref, own_ref):
    wt = wt_ref[...]
    for i in range(4):
        for side in range(2):
            unit, _ = norm_rows(pair_ref[i, 128 * side : 128 * side + 128, :].astype(F32))
            both = mm(wt, (unit * gain_ref[...]).astype(BF16), NT)
            at = 8 * i + 4 * side
            for r in range(BI):
                own_ref[r, at : at + 4, :] = both[0:4]
                own_ref[r, 32 + at : 36 + at, :] = both[4:8]


def pair_bias(pair, gain, wt):
    return pl.pallas_call(
        pair_bias_kernel,
        out_shape=jax.ShapeDtypeStruct((BI, 64, 128), F32),
        compiler_params=pltpu.CompilerParams(vmem_limit_bytes=56 * MIB),
        cost_estimate=TINY,
        name="pair_bias",
    )(pair, gain, wt)


def pair_sums_kernel(parts_ref, small_ref, normed_ref, wt_ref, block_ref, mine_ref):
    mine = jnp.sum(parts_ref[...].astype(F32), axis=0)
    mine_ref[...] = mine[0:64]
    tiles = []
    for tile in range(8):
        at = 4 * tile
        tiles.append(jnp.concatenate([mine[at : at + 4], mine[32 + at : 36 + at]], axis=0))
    d_bias = jnp.concatenate(tiles, axis=1)
    high = d_bias.astype(BF16).astype(F32)
    pieces = jnp.concatenate([high, d_bias - high], axis=0).astype(BF16)
    both = mm(pieces, normed_ref[...])
    both = both[0:8] + both[8:16]
    d_pg = jnp.sum((both[:, 128:256] + both[:, 256:384]) * wt_ref[...].astype(F32), axis=0, keepdims=True)
    block_ref[0:40, :] = mine[64:104]
    block_ref[40:48, :] = jnp.concatenate([small_ref[0:6, :], d_pg, small_ref[7:8, :]], axis=0)
    block_ref[48:56, :] = both[:, 0:128]


def pair_sums(parts, small, normed, wt):
    return pl.pallas_call(
        pair_sums_kernel,
        out_shape=[
            jax.ShapeDtypeStruct((56, 128), F32),
            jax.ShapeDtypeStruct((64, 128), F32),
        ],
        compiler_params=pltpu.CompilerParams(vmem_limit_bytes=8 * MIB),
        cost_estimate=TINY,
        name="pair_sums",
    )(parts, small, normed, wt)


def pair_grad_kernel(mine_ref, pair_ref, gain_ref, wt_ref, dpair_ref):
    wt = jnp.concatenate([wt_ref[...].astype(F32)] * 2, axis=0).astype(BF16)
    gain = gain_ref[...]
    for i in range(4):
        for side in range(2):
            here = slice(128 * side, 128 * side + 128)
            at = 8 * i + 4 * side
            d_bias = jnp.concatenate([mine_ref[at : at + 4, :], mine_ref[32 + at : 36 + at, :]], axis=0)
            high = d_bias.astype(BF16).astype(F32)
            pieces = jnp.concatenate([high, d_bias - high], axis=0)
            unit, inverse = norm_rows(pair_ref[i, here, :].astype(F32))
            g = mm(pieces.T.astype(BF16), wt) * gain
            mean = jnp.mean(g, axis=-1, keepdims=True)
            cross = jnp.mean(g * unit, axis=-1, keepdims=True)
            dpair_ref[i, here, :] = (inverse * (g - mean - unit * cross)).astype(BF16)


def pair_grad(mine, pair, gain, wt):
    return pl.pallas_call(
        pair_grad_kernel,
        out_shape=jax.ShapeDtypeStruct((4, 256, 128), BF16),
        compiler_params=pltpu.CompilerParams(vmem_limit_bytes=8 * MIB),
        cost_estimate=TINY,
        name="pair_grad",
    )(mine, pair, gain, wt)


def exchange(blocks, axes):
    return lax.all_to_all(blocks, axes, 0, 0, tiled=True)


def spread(block, count, axes):
    return exchange(jnp.broadcast_to(block[None], (count,) + block.shape), axes)


def local(x, pair, adj, w, gbias, wo, gain, shift, pair_gain, pair_w):
    x, adj, pair = x[0], adj[0], pair[0]
    gain2, shift2 = gain.reshape(1, 256), shift.reshape(1, 256)
    pair_gain2 = pair_gain.reshape(1, 128)
    pair_wt = pair_w.T
    column = exchange(pair_bias(pair, pair_gain2, pair_wt), BIAS_INNER)
    bias_a = spread(column[:, :32], BO, BIAS_OUTER).reshape(2048, 128)
    *made, copies = project(x, adj, w, wo, gain2, shift2, gbias.reshape(1, 256), column)
    bias_b = exchange(copies, BIAS_OUTER).reshape(2048, 128)

    dp_a, gb_a, send_a, grad_a = attend(bias_a, *made, adj, 0, None)
    dp_b, gb_b, send_b = attend(bias_b, *made, adj, 1, grad_a)
    dx, small, normed = inputs_grad(x, w, gain2, dp_a, dp_b, gb_a, gb_b, pair, pair_gain2)

    first, second = (exchange(t.reshape(GO, GI, -1, 128), GRAD_OUTER) for t in (send_a, send_b))
    first, second = (jnp.sum(t.astype(F32), axis=0).astype(BF16) for t in (first, second))
    order = [first[:, :32], second[:, :32], first[:, 32:], second[:, 32:]]
    parts = exchange(jnp.concatenate(order, axis=1), GRAD_INNER)
    block, mine = pair_sums(parts, small, normed, pair_wt)
    dpair = pair_grad(mine, pair, pair_gain2, pair_wt)
    others = [
        lax.ppermute(block, ("x_lo", "core"), [(n, n ^ flip) for n in range(4)]) for flip in (1, 2, 3)
    ]
    block = (block + others[0]) + (others[1] + others[2])
    line = spread(block.astype(BF16), RI, BACK_INNER)
    tail = jnp.sum(line[:, 40:].astype(F32), axis=0).astype(BF16)
    total = spread(jnp.concatenate([line[:, :40].reshape(40 * RI, 128), tail], axis=0), RO, BACK_OUTER)
    dw, dwo, gb, mg, mb, pg, wb = unpack(total)
    return (
        dx[None],
        dpair[None],
        dw,
        gb.reshape(256),
        dwo,
        mg.reshape(256),
        mb.reshape(256),
        pg.reshape(128),
        wb.T,
    )


def solution(mesh):
    fine = Mesh(mesh.devices.reshape(2, 2, 4, 8, 2), ("x_lo", "core", "y", "z", "x_hi"))
    split = P(("x_lo", "core"), AXIAL)
    return jax.shard_map(
        local,
        mesh=fine,
        in_specs=(split,) * 3 + (P(),) * 7,
        out_specs=(split, split) + (P(),) * 7,
        check_vma=False,
    )
```

```python
import jax
import jax.numpy as jnp
from jax import lax
from jax.experimental import pallas as pl
from jax.experimental.pallas import tpu as pltpu
from jax.sharding import Mesh, PartitionSpec as P

EPS = 1e-05
F32 = jnp.float32
BF16 = jnp.bfloat16
AXIAL = ("y", "z", "x_hi")
BIAS_INNER, BIAS_OUTER = ("z",), ("y", "x_hi")
GRAD_INNER, GRAD_OUTER = ("z", "x_hi"), ("y",)
BACK_INNER, BACK_OUTER = ("z",), ("y", "x_hi")
SIZES = {"y": 4, "z": 8, "x_hi": 2}


def count(axes):
    total = 1
    for axis in axes:
        total *= SIZES[axis]
    return total


def places(outer, inner):
    result = []
    for y in range(4):
        for z in range(8):
            for x in range(2):
                place = 0
                for axis in outer + inner:
                    place = place * SIZES[axis] + {"y": y, "z": z, "x_hi": x}[axis]
                result.append(place)
    return result


BIAS_SENT = places(BIAS_OUTER, BIAS_INNER)
GRAD_SENT = places(GRAD_OUTER, GRAD_INNER)
BACK_SENT = places(BACK_OUTER, BACK_INNER)
BI, BO, GI, GO = (count(axes) for axes in (BIAS_INNER, BIAS_OUTER, GRAD_INNER, GRAD_OUTER))
RI, RO = count(BACK_INNER), count(BACK_OUTER)
TINY = pl.CostEstimate(flops=1000, bytes_accessed=1000, transcendentals=0)
FIRST = [(side, 8 * n) for side in range(2) for n in range(64)]
SECOND = [(0, side, 8 * n) for side in range(2) for n in range(64, 80)]
SECOND += [(1, side, 8 * n) for side in range(2) for n in range(80)]


def packed_row(chunk, side, row):
    return 1280 * side + 256 * (row // 128) + 128 * chunk + row % 128


GROUPS = [
    [packed_row(0, *g) for g in FIRST[2 * d : 2 * d + 2]] + [packed_row(*g) for g in SECOND[3 * d : 3 * d + 3]]
    for d in range(64)
]
MIB = 1024 * 1024

NN = (((1,), (0,)), ((), ()))
NT = (((1,), (1,)), ((), ()))


def mm(a, b, dims=NN):
    return lax.dot_general(a, b, dims, preferred_element_type=F32)


def norm_rows(x):
    average = jnp.mean(x, axis=-1, keepdims=True)
    centered = x - average
    inverse = lax.rsqrt(jnp.mean(centered * centered, axis=-1, keepdims=True) + EPS)
    return centered * inverse, inverse


def project_kernel(
    x_ref, adj_ref, w_ref, wo_ref, gain_ref, shift_ref, gbias_ref, column_ref,
    qt_ref, kt_ref, vt_ref, k_ref, v_ref, gt_ref, dat_ref, xn_ref, copies_ref, wt_ref, gcol_ref,
):
    @pl.when(pl.program_id(0) == 0)
    def _():
        wt_ref[...] = w_ref[...].astype(F32).T.astype(BF16)
        gcol_ref[...] = jnp.broadcast_to(gbias_ref[...], (128, 256)).T
        for r in range(BO):
            for z in range(BI):
                copies_ref[r, 32 * z : 32 * z + 32, :] = column_ref[z, 32:64, :]

    unit, _ = norm_rows(x_ref[...].reshape(512, 256).astype(F32))
    xn = (unit * gain_ref[...] + shift_ref[...]).astype(BF16)
    xn_ref[...] = xn.reshape(2, 256, 256)
    k_ref[...] = mm(xn, w_ref[:, 256:512]).astype(BF16).reshape(2, 256, 256)
    v_ref[...] = mm(xn, w_ref[:, 512:768]).astype(BF16).reshape(2, 256, 256)
    factor = 32 ** (-0.5)
    shifted = jnp.concatenate([gcol_ref[...], gcol_ref[...]], axis=1)
    for r in range(2):
        row = xn[256 * r : 256 * r + 256]
        qt_ref[r] = (mm(wt_ref[0:256, :], row, NT) * factor).astype(BF16)
        kt_ref[r] = mm(wt_ref[256:512, :], row, NT).astype(BF16)
        vt_ref[r] = mm(wt_ref[512:768, :], row, NT).astype(BF16)
        gate = jax.nn.sigmoid(mm(wt_ref[768:1024, :], row, NT) + shifted)
        dgated = mm(wo_ref[...], adj_ref[r], NT)
        gt_ref[r] = gate
        dat_ref[r] = (dgated * gate).astype(BF16)


def project(x, adj, w, wo, gain, shift, gbias, column):
    rows = x.shape[0]
    block = pl.BlockSpec((2, 256, 256), lambda s: (s, 0, 0))
    whole = lambda a: pl.BlockSpec(a.shape, lambda s: (0,) * a.ndim)
    small = jax.ShapeDtypeStruct((rows, 256, 256), BF16)
    big = jax.ShapeDtypeStruct((rows, 256, 256), F32)
    return pl.pallas_call(
        project_kernel,
        grid=(rows // 2,),
        in_specs=[block, block, whole(w), whole(wo), whole(gain), whole(shift), whole(gbias), whole(column)],
        out_specs=[block] * 8 + [pl.BlockSpec((BO, 32 * BI, 128), lambda s: (0, 0, 0))],
        out_shape=[small] * 5 + [big, small, small, jax.ShapeDtypeStruct((BO, 32 * BI, 128), F32)],
        scratch_shapes=[pltpu.VMEM((1024, 256), BF16), pltpu.VMEM((256, 128), F32)],
        compiler_params=pltpu.CompilerParams(vmem_limit_bytes=56 * MIB),
        cost_estimate=TINY,
        name="project",
    )(x, adj, w, wo, gain, shift, gbias, column)


def attend_kernel(
    heads, rows, last,
    bias_ref, qt_ref, kt_ref, vt_ref, k_ref, v_ref, gt_ref, dat_ref, xn_ref, adj_ref, *refs
):
    if last:
        other_ref, dp_ref, gb_ref, send_ref, bt_ref, acc_ref, out_ref, w_ref, stage_ref = refs
    else:
        dp_ref, gb_ref, send_ref, grad_ref, bt_ref, acc_ref, out_ref, w_ref, stage_ref = refs
    step = pl.program_id(0)
    width = 32 * heads

    @pl.when(step == 0)
    def _():
        for natural, sent in enumerate(BIAS_SENT):
            out_ref[32 * natural : 32 * natural + 32, :] = bias_ref[32 * sent : 32 * sent + 32, :]
        for h in range(heads):
            for side in range(2):
                part = out_ref[pl.ds(side * heads + h, 256, stride=2 * heads), :]
                bt_ref[h, 128 * side : 128 * side + 128, :] = part.T
        acc_ref[...] = jnp.zeros_like(acc_ref)
        gb_ref[...] = jnp.zeros_like(gb_ref)
        w_ref[...] = jnp.zeros_like(w_ref)

    def own(block, at):
        parts = []
        if at:
            parts.append(jnp.zeros((32 * at, 256), BF16))
        parts.append(block)
        if at < 3:
            parts.append(jnp.zeros((32 * (3 - at), 256), BF16))
        return jnp.concatenate(parts, axis=0)

    gated = [[] for _ in range(2)]

    def place(h):
        return slice(32 * h, 32 * h + 32)

    def score(r, h):
        here = place(h)
        st = mm(k_ref[r], own(qt_ref[r, here, :], h))
        dpt = mm(v_ref[r], own(dat_ref[r, here, :], h))
        return st, dpt

    def soft(r, h, st, dpt):
        st = st + bt_ref[h]
        e = jnp.exp(st - jnp.max(st, axis=0, keepdims=True))
        p = e * (1.0 / jnp.sum(e, axis=0, keepdims=True))
        delta = jnp.sum(p * dpt, axis=0, keepdims=True)
        ds = p * (dpt - delta)
        acc_ref[h] += ds
        return p.astype(BF16), ds.astype(BF16)

    def half_soft(r, h, st, dpt):
        ps, dss = [], []
        for side in range(2):
            at = slice(128 * side, 128 * side + 128)
            x = st[:, at] + bt_ref[h, :, at]
            e = jnp.exp(x - jnp.max(x, axis=0, keepdims=True))
            p = e * (1.0 / jnp.sum(e, axis=0, keepdims=True))
            d = dpt[:, at]
            delta = jnp.sum(p * d, axis=0, keepdims=True)
            ds = p * (d - delta)
            acc_ref[h, :, at] += ds
            ps.append(p.astype(BF16))
            dss.append(ds.astype(BF16))
        return jnp.concatenate(ps, axis=1), jnp.concatenate(dss, axis=1)

    def close(r, h, p_low, ds_low):
        here = place(h)
        out = slice(32 * h, 32 * h + 32)
        att = mm(vt_ref[r, here, :], p_low)
        g = gt_ref[r, here, :]
        graw = dat_ref[r, here, :].astype(F32) * att * (1.0 - g)
        gated[r].append((g * att).astype(BF16))
        gb_ref[out, :] += graw[:, :128] + graw[:, 128:]
        dp_ref[r, 0, out, :] = (mm(kt_ref[r, here, :], ds_low) * (32 ** (-0.5))).astype(BF16)
        dp_ref[r, 1, out, :] = mm(qt_ref[r, here, :], ds_low, NT).astype(BF16)
        dp_ref[r, 2, out, :] = mm(dat_ref[r, here, :], p_low, NT).astype(BF16)
        dp_ref[r, 3, out, :] = graw.astype(BF16)

    items = [(r, h) for r in range(2) for h in range(heads)]
    scores = [score(*items[0])]
    lows = []
    for n, item in enumerate(items):
        if n + 1 < len(items):
            scores.append(score(*items[n + 1]))
        lows.append(half_soft(*item, *scores[n]))
        if n:
            close(*items[n - 1], *lows[n - 1])
    close(*items[-1], *lows[-1])

    xn = xn_ref[...].reshape(256 * 2, 256)
    for b in range(4):
        both = jnp.concatenate([dp_ref[r, b] for r in range(2)], axis=1)
        w_ref[width * b : width * b + width, :] += mm(both, xn)
    both = jnp.concatenate([jnp.concatenate(g, axis=0) for g in gated], axis=1)
    w_ref[4 * width : 5 * width, :] += mm(both, adj_ref[...].reshape(256 * 2, 256))

    @pl.when(step == rows // 2 - 1)
    def _():
        for h in range(heads):
            for side in range(2):
                part = acc_ref[h, 128 * side : 128 * side + 128, :]
                out_ref[pl.ds(side * heads + h, 256, stride=2 * heads), :] = part.T
        for natural, sent in enumerate(GRAD_SENT):
            stage_ref[sent, 0:32, :] = out_ref[32 * natural : 32 * natural + 32, :]
        if not last:
            for n, (side, row) in enumerate(FIRST):
                to = 32 + 8 * (n % 2)
                stage_ref[n // 2, to : to + 8, :] = w_ref[row : row + 8, 128 * side : 128 * side + 128]
            for side in range(2):
                grad_ref[side] = w_ref[512:640, 128 * side : 128 * side + 128]
        else:
            for n, (c, side, row) in enumerate(SECOND):
                to = 32 + 8 * (n % 3)
                if c:
                    piece = w_ref[row : row + 8, 128 * side : 128 * side + 128]
                else:
                    piece = other_ref[side, row - 512 : row - 504, :]
                stage_ref[n // 3, to : to + 8, :] = piece
        send_ref[...] = stage_ref[...].astype(BF16)


def attend(bias, qt, kt, vt, k, v, gt, dat, xn, adj, chunk, other):
    rows, heads = qt.shape[0], 4
    last = other is not None
    block = pl.BlockSpec((2, 256, 256), lambda s: (s, 0, 0))
    width = 32 * heads

    def kernel(*refs):
        attend_kernel(heads, rows, last, *refs)

    half = pl.BlockSpec((2, width, 256), lambda s: (s, chunk, 0))
    columns = pl.BlockSpec((2, 256, width), lambda s: (s, 0, chunk))
    in_specs = [pl.BlockSpec((512 * heads, 128), lambda s: (0, 0))]
    in_specs += [half, half, half, columns, columns, half, half, block, block]
    out_specs = [
        pl.BlockSpec((2, 4, width, 256), lambda s: (s, 0, 0, 0)),
        pl.BlockSpec((width, 128), lambda s: (0, 0)),
    ]
    out_shape = [
        jax.ShapeDtypeStruct((rows, 4, width, 256), BF16),
        jax.ShapeDtypeStruct((width, 128), F32),
    ]
    scratch = [
        pltpu.VMEM((heads, 256, 256), F32),
        pltpu.VMEM((heads, 256, 256), F32),
        pltpu.VMEM((512 * heads, 128), F32),
        pltpu.VMEM((5 * width, 256), F32),
    ]
    operands = [bias, qt, kt, vt, k, v, gt, dat, xn, adj]
    height = 8 * heads + (24 if last else 16)
    out_specs.append(pl.BlockSpec((64, height, 128), lambda s: (0, 0, 0)))
    out_shape.append(jax.ShapeDtypeStruct((64, height, 128), BF16))
    scratch.append(pltpu.VMEM((64, height, 128), F32))
    rest = pl.BlockSpec((2, width, 128), lambda s: (0, 0, 0))
    if last:
        in_specs.append(rest)
        operands.append(other)
    else:
        out_specs.append(rest)
        out_shape.append(jax.ShapeDtypeStruct((2, width, 128), F32))
    return pl.pallas_call(
        kernel,
        grid=(rows // 2,),
        in_specs=in_specs,
        out_specs=out_specs,
        out_shape=out_shape,
        scratch_shapes=scratch,
        compiler_params=pltpu.CompilerParams(vmem_limit_bytes=56 * MIB),
        cost_estimate=TINY,
        name="attend",
    )(*operands)


def inputs_kernel(
    rows, x_ref, w_ref, gain_ref, dpa_ref, dpb_ref, gba_ref, gbb_ref, pair_ref, pgain_ref,
    dx_ref, small_ref, normed_ref, mg_ref, mb_ref,
):
    step = pl.program_id(0)

    @pl.when(step == 0)
    def _():
        mg_ref[...] = jnp.zeros_like(mg_ref)
        mb_ref[...] = jnp.zeros_like(mb_ref)

    pair_unit, _ = norm_rows(pair_ref[0].astype(F32))
    high = pair_unit.astype(BF16)
    normed_ref[:, 0:128] = (pair_unit * pgain_ref[...]).astype(BF16)
    normed_ref[:, 128:256] = high
    normed_ref[:, 256:384] = (pair_unit - high.astype(F32)).astype(BF16)

    unit, inverse = norm_rows(x_ref[0].astype(F32))
    gain = gain_ref[...]
    dp = jnp.concatenate([r[0, b] for b in range(4) for r in (dpa_ref, dpb_ref)], axis=0)
    dn = mm(w_ref[...], dp).T
    mg_ref[...] += jnp.sum(unit * dn, axis=0, keepdims=True)
    mb_ref[...] += jnp.sum(dn, axis=0, keepdims=True)
    g = dn * gain
    mean = jnp.mean(g, axis=-1, keepdims=True)
    cross = jnp.mean(g * unit, axis=-1, keepdims=True)
    dx_ref[0] = (inverse * (g - mean - unit * cross)).astype(BF16)

    @pl.when(step == rows - 1)
    def _():
        gb = [jnp.sum(r[...].T, axis=0, keepdims=True) for r in (gba_ref, gbb_ref)]
        mg, mb = mg_ref[...], mb_ref[...]
        small_ref[...] = jnp.concatenate(
            gb + [mg[:, :128], mg[:, 128:], mb[:, :128], mb[:, 128:], jnp.zeros((2, 128), F32)], axis=0
        )


def inputs_grad(x, w, gain, dp_a, dp_b, gb_a, gb_b, pair, pair_gain):
    rows = x.shape[0]
    block = pl.BlockSpec((1, 256, 256), lambda s: (s, 0, 0))
    quad = pl.BlockSpec((1, 4, 128, 256), lambda s: (s, 0, 0, 0))
    whole = lambda a: pl.BlockSpec(a.shape, lambda s: (0,) * a.ndim)

    def kernel(*refs):
        inputs_kernel(rows, *refs)

    return pl.pallas_call(
        kernel,
        grid=(rows,),
        in_specs=[
            block, whole(w), whole(gain), quad, quad, whole(gb_a), whole(gb_b),
            pl.BlockSpec((1, 128, 128), lambda s: (s // 2, s % 2, 0)), whole(pair_gain),
        ],
        out_specs=[
            block,
            pl.BlockSpec((8, 128), lambda s: (0, 0)),
            pl.BlockSpec((128, 384), lambda s: (s, 0)),
        ],
        out_shape=[
            jax.ShapeDtypeStruct((rows, 256, 256), BF16),
            jax.ShapeDtypeStruct((8, 128), F32),
            jax.ShapeDtypeStruct((1024, 384), BF16),
        ],
        scratch_shapes=[pltpu.VMEM((1, 256), F32), pltpu.VMEM((1, 256), F32)],
        compiler_params=pltpu.CompilerParams(vmem_limit_bytes=56 * MIB),
        cost_estimate=TINY,
        name="inputs_grad",
    )(x, w, gain, dp_a, dp_b, gb_a, gb_b, pair, pair_gain)


def unpack_kernel(total_ref, dw_ref, dwo_ref, gb_ref, mg_ref, mb_ref, pg_ref, wb_ref, all_ref, main_ref):
    f = float(524288) ** (-0.5)
    fp = float(262144) ** (-0.5)
    all_ref[...] = total_ref[...].astype(F32)
    for sent, back in zip(GRAD_SENT, BACK_SENT):
        for k, row in enumerate(GROUPS[sent]):
            at = 40 * (back % RI) + 8 * k
            main_ref[row : row + 8, :] = all_ref[back // RI, at : at + 8, :] * f
    for side in range(2):
        lanes = slice(128 * side, 128 * side + 128)
        base = 1280 * side
        dw_ref[lanes, :] = main_ref[base : base + 1024, :].T
        dwo_ref[:, lanes] = main_ref[base + 1024 : base + 1280, :]
    tail = jnp.sum(all_ref[:, 40 * RI :, :], axis=0)
    for n, ref in enumerate((gb_ref, mg_ref, mb_ref)):
        ref[...] = jnp.concatenate([tail[2 * n : 2 * n + 1], tail[2 * n + 1 : 2 * n + 2]], axis=1) * f
    pg_ref[...] = tail[6:7] * fp
    wb_ref[...] = tail[8:16] * fp


def unpack(total):
    vector = jax.ShapeDtypeStruct((1, 256), F32)
    return pl.pallas_call(
        unpack_kernel,
        out_shape=[
            jax.ShapeDtypeStruct((256, 1024), F32),
            jax.ShapeDtypeStruct((256, 256), F32),
            vector, vector, vector,
            jax.ShapeDtypeStruct((1, 128), F32),
            jax.ShapeDtypeStruct((8, 128), F32),
        ],
        scratch_shapes=[pltpu.VMEM((RO, 40 * RI + 16, 128), F32), pltpu.VMEM((2560, 128), F32)],
        compiler_params=pltpu.CompilerParams(vmem_limit_bytes=12 * MIB),
        cost_estimate=TINY,
        name="unpack",
    )(total)


def pair_bias_kernel(pair_ref, gain_ref, wt_ref, own_ref):
    wt = wt_ref[...]
    for i in range(4):
        for side in range(2):
            unit, _ = norm_rows(pair_ref[i, 128 * side : 128 * side + 128, :].astype(F32))
            both = mm(wt, (unit * gain_ref[...]).astype(BF16), NT)
            at = 8 * i + 4 * side
            for r in range(BI):
                own_ref[r, at : at + 4, :] = both[0:4]
                own_ref[r, 32 + at : 36 + at, :] = both[4:8]


def pair_bias(pair, gain, wt):
    return pl.pallas_call(
        pair_bias_kernel,
        out_shape=jax.ShapeDtypeStruct((BI, 64, 128), F32),
        compiler_params=pltpu.CompilerParams(vmem_limit_bytes=56 * MIB),
        cost_estimate=TINY,
        name="pair_bias",
    )(pair, gain, wt)


def pair_sums_kernel(parts_ref, small_ref, normed_ref, wt_ref, block_ref, mine_ref):
    mine = jnp.sum(parts_ref[...].astype(F32), axis=0)
    mine_ref[...] = mine[0:64]
    tiles = []
    for tile in range(8):
        at = 4 * tile
        tiles.append(jnp.concatenate([mine[at : at + 4], mine[32 + at : 36 + at]], axis=0))
    d_bias = jnp.concatenate(tiles, axis=1)
    high = d_bias.astype(BF16).astype(F32)
    pieces = jnp.concatenate([high, d_bias - high], axis=0).astype(BF16)
    both = mm(pieces, normed_ref[...])
    both = both[0:8] + both[8:16]
    d_pg = jnp.sum((both[:, 128:256] + both[:, 256:384]) * wt_ref[...].astype(F32), axis=0, keepdims=True)
    block_ref[0:40, :] = mine[64:104]
    block_ref[40:48, :] = jnp.concatenate([small_ref[0:6, :], d_pg, small_ref[7:8, :]], axis=0)
    block_ref[48:56, :] = both[:, 0:128]


def pair_sums(parts, small, normed, wt):
    return pl.pallas_call(
        pair_sums_kernel,
        out_shape=[
            jax.ShapeDtypeStruct((56, 128), F32),
            jax.ShapeDtypeStruct((64, 128), F32),
        ],
        compiler_params=pltpu.CompilerParams(vmem_limit_bytes=8 * MIB),
        cost_estimate=TINY,
        name="pair_sums",
    )(parts, small, normed, wt)


def pair_grad_kernel(mine_ref, pair_ref, gain_ref, wt_ref, dpair_ref):
    wt = jnp.concatenate([wt_ref[...].astype(F32)] * 2, axis=0).astype(BF16)
    gain = gain_ref[...]
    for i in range(4):
        for side in range(2):
            here = slice(128 * side, 128 * side + 128)
            at = 8 * i + 4 * side
            d_bias = jnp.concatenate([mine_ref[at : at + 4, :], mine_ref[32 + at : 36 + at, :]], axis=0)
            high = d_bias.astype(BF16).astype(F32)
            pieces = jnp.concatenate([high, d_bias - high], axis=0)
            unit, inverse = norm_rows(pair_ref[i, here, :].astype(F32))
            g = mm(pieces.T.astype(BF16), wt) * gain
            mean = jnp.mean(g, axis=-1, keepdims=True)
            cross = jnp.mean(g * unit, axis=-1, keepdims=True)
            dpair_ref[i, here, :] = (inverse * (g - mean - unit * cross)).astype(BF16)


def pair_grad(mine, pair, gain, wt):
    return pl.pallas_call(
        pair_grad_kernel,
        out_shape=jax.ShapeDtypeStruct((4, 256, 128), BF16),
        compiler_params=pltpu.CompilerParams(vmem_limit_bytes=8 * MIB),
        cost_estimate=TINY,
        name="pair_grad",
    )(mine, pair, gain, wt)


def exchange(blocks, axes):
    return lax.all_to_all(blocks, axes, 0, 0, tiled=True)


def spread(block, count, axes):
    return exchange(jnp.broadcast_to(block[None], (count,) + block.shape), axes)


def local(x, pair, adj, w, gbias, wo, gain, shift, pair_gain, pair_w):
    x, adj, pair = x[0], adj[0], pair[0]
    gain2, shift2 = gain.reshape(1, 256), shift.reshape(1, 256)
    pair_gain2 = pair_gain.reshape(1, 128)
    pair_wt = pair_w.T
    column = exchange(pair_bias(pair, pair_gain2, pair_wt), BIAS_INNER)
    bias_a = spread(column[:, :32], BO, BIAS_OUTER).reshape(2048, 128)
    *made, copies = project(x, adj, w, wo, gain2, shift2, gbias.reshape(1, 256), column)
    bias_b = exchange(copies, BIAS_OUTER).reshape(2048, 128)

    dp_a, gb_a, send_a, grad_a = attend(bias_a, *made, adj, 0, None)
    dp_b, gb_b, send_b = attend(bias_b, *made, adj, 1, grad_a)
    dx, small, normed = inputs_grad(x, w, gain2, dp_a, dp_b, gb_a, gb_b, pair, pair_gain2)

    first, second = (exchange(t.reshape(GO, GI, -1, 128), GRAD_OUTER) for t in (send_a, send_b))
    first, second = (jnp.sum(t.astype(F32), axis=0).astype(BF16) for t in (first, second))
    order = [first[:, :32], second[:, :32], first[:, 32:], second[:, 32:]]
    parts = exchange(jnp.concatenate(order, axis=1), GRAD_INNER)
    block, mine = pair_sums(parts, small, normed, pair_wt)
    dpair = pair_grad(mine, pair, pair_gain2, pair_wt)
    others = [
        lax.ppermute(block, ("x_lo", "core"), [(n, n ^ flip) for n in range(4)]) for flip in (1, 2, 3)
    ]
    block = (block + others[0]) + (others[1] + others[2])
    line = spread(block.astype(BF16), RI, BACK_INNER)
    tail = jnp.sum(line[:, 40:].astype(F32), axis=0).astype(BF16)
    total = spread(jnp.concatenate([line[:, :40].reshape(40 * RI, 128), tail], axis=0), RO, BACK_OUTER)
    dw, dwo, gb, mg, mb, pg, wb = unpack(total)
    return (
        dx[None],
        dpair[None],
        dw,
        gb.reshape(256),
        dwo,
        mg.reshape(256),
        mb.reshape(256),
        pg.reshape(128),
        wb.T,
    )


def solution(mesh):
    fine = Mesh(mesh.devices.reshape(2, 2, 4, 8, 2), ("x_lo", "core", "y", "z", "x_hi"))
    split = P(("x_lo", "core"), AXIAL)
    return jax.shard_map(
        local,
        mesh=fine,
        in_specs=(split,) * 3 + (P(),) * 7,
        out_specs=(split, split) + (P(),) * 7,
        check_vma=False,
    )
```
